512 devices in a mesh: dp: 64 (over z, x, y_hi), tensor: 8 (over y_lo, core).
Axes of the slice: x: 4, y: 8 (y_hi: 2, y_lo: 4; y = y_hi * 4 + y_lo), z: 8, core: 2. Of those that a mesh axis runs over, the one named last changes fastest.
Arguments:
- context: bfloat16 [32768, 2048], P('dp', 'tensor'), may hold values from -6 to 6
- residual: bfloat16 [32768, 4096], P('dp', 'tensor'), may hold values from -6 to 6
- out_weight: bfloat16 [2048, 4096], P(None, 'tensor'), may hold values from -0.125 to 0.125
- final_norm_weight: float32 [4096], P('tensor'), may hold values from 0.25 to 1.75
- query_lengths: int32 [1024], P('dp'), may hold values from 1 to 16, 8192 in all
- passage_lengths: int32 [1024], P('dp'), may hold values from 1 to 16, 8192 in all
- positive_index: int32 [1024], P('dp'), may hold values from 0 to 1023
- tile_mask: int32 [8, 8], replicated, may hold values 0 or 1
Outputs:
- query_loss: float32 [1024], P(('dp', 'tensor'))
- residual_gradient: bfloat16 [32768, 4096], P('dp', 'tensor')
- d_context: bfloat16 [32768, 2048], P('dp', 'tensor')
The draws below stay inside these ranges and needn't reach their ends.
Inputs may be any that keep to these rules, and one draw needn't show every extreme that they name: `query_lengths`: tokens past a query's length are padding. `passage_lengths`: tokens past a passage's length are padding.
All inputs are finite; a program needn't handle non-finite values. No bound on the sum of `query_lengths` or of `passage_lengths` on one device may be relied on, other than what follows from the above.
Results may differ from the reference program's by a relative error of at most 0.023.
Values may be sent and summed in bfloat16 or wider, within the bound.
No kernel may reach another device: no remote copies, remote signals or barrier semaphores. Data moves between devices by JAX's collectives and lax.ppermute only.
A program may use at most 64 MiB of HBM per device.

```python
import math
import jax
import jax.numpy as jnp
import numpy as np
from jax import lax

D = 4096
Q_DEV = 16
P_DEV = 16
SEQ_LEN = 16
TILE = 128
HW = 2048
TOKENS = 32768
QUERIES = 1024
PASSAGES = 1024
Q_TILES = 8
P_TILES = 8
N_DP = 64
N_TENSOR = 8


def with_ends(drawn, stream_key, low, top_value):
    index_at = [jax.random.randint(jax.random.fold_in(stream_key, axis), (), 0, length) for axis, length in enumerate(drawn.shape)]
    widest = drawn.shape.index(max(drawn.shape))
    next_to = index_at[:widest] + [(index_at[widest] + 1) % drawn.shape[widest]] + index_at[widest + 1:]
    return drawn.at[tuple(index_at)].set(low).at[tuple(next_to)].set(top_value)


def steps_of(rng, dims, split, smallest, high):
    def one(position, shards_of):
        steps = jax.random.uniform(jax.random.fold_in(jax.random.fold_in(rng, 6), position), (shards_of,), jnp.float32, smallest / len(split), high / len(split))
        return jnp.repeat(jnp.exp(steps), dims[position] // shards_of).reshape((-1,) + (1,) * (len(dims) - position - 1))

    gain = one(*split[0])
    for cut in split[1:]:
        gain = gain * one(*cut)
    return gain


def profile(count, total, most, slope):
    weights = [(1 << 20) // math.isqrt(grade ** slope) + 1 for grade in range(2, count + 1)]
    surplus, counts = total - most - (count - 1), [1] * (count - 1)
    while surplus > 0:
        free = [i for i in range(count - 1) if counts[i] < most]
        pool, left = sum([weights[i] for i in free]), surplus
        for i in free:
            addition = min(most - counts[i], max(1, left * weights[i] // pool), surplus)
            counts[i] = counts[i] + addition
            surplus = surplus - addition
    return np.array([most] + counts)


def uneven_parts(key, number_of, total, bound, skew):
    if number_of == 2:
        one = jax.random.randint(key, (), max(1, total - bound), min(bound, total - 1) + 1)
        return jnp.stack([one, total - one])
    sizes = jnp.asarray(profile(number_of, total, bound, skew), jnp.int32)
    twos = (number_of - 1) // 2
    donor, receiver = sizes[1:1 + 2 * twos:2], sizes[2:2 + 2 * twos:2]
    slack = jnp.minimum(donor - 1, bound - receiver)
    moved = jax.random.randint(jax.random.fold_in(key, 1), (twos,), 0, 1 << 20) % (slack + 1)
    sizes = sizes.at[1:1 + 2 * twos:2].set(donor - moved).at[2:2 + 2 * twos:2].set(receiver + moved)
    return sizes[jax.random.permutation(jax.random.fold_in(key, 2), number_of)]


def centred(key, shape, width, limit, split=(), held_as=jnp.bfloat16):
    level = steps_of(key, shape, split, -0.22, 0.18) if split else 1.0
    values = jax.random.normal(key, shape, jnp.float32) * width * level
    return jnp.minimum(jnp.maximum(values, -limit), limit).astype(held_as)


def setup_inputs(seed: int = 0) -> dict:
    key_of = jax.random.split(jax.random.key(seed), 9)
    return {
        "context": centred(key_of[0], (TOKENS, HW), 1.0, 6.0, ((0, 64), (1, 8))),
        "residual": centred(key_of[1], (TOKENS, D), 1.0, 6.0, ((0, 64), (1, 8))),
        "out_weight": centred(key_of[2], (HW, D), HW ** -0.5, 0.125, ((1, 8),)),
        "final_norm_weight": jnp.clip(1.0 + 0.15 * jax.random.normal(key_of[3], (D,), jnp.float32), 0.25, 1.75),
        "query_lengths": uneven_parts(key_of[4], QUERIES, QUERIES * SEQ_LEN // 2, SEQ_LEN, 0).astype(jnp.int32),
        "passage_lengths": uneven_parts(key_of[5], PASSAGES, PASSAGES * SEQ_LEN // 2, SEQ_LEN, 0).astype(jnp.int32),
        "positive_index": with_ends(jax.random.randint(key_of[6], (QUERIES,), 0, PASSAGES), jax.random.fold_in(key_of[6], 1), 0, PASSAGES - 1).astype(jnp.int32),
        "tile_mask": with_ends((jax.random.randint(key_of[7], (Q_TILES, P_TILES), 0, 2) < 1).astype(jnp.int32), jax.random.fold_in(key_of[7], 1), 0, 1),
    }


EPS = 1e-06
LOGIT_SCALE = 20.0
LOSS_SCALE = 1024.0

def reference(context, residual, out_weight, final_norm_weight, query_lengths, passage_lengths, positive_index, tile_mask):
    f32 = jnp.float32
    seqs = Q_DEV + P_DEV
    hidden_state = residual.astype(f32) + jnp.dot(context, out_weight, preferred_element_type=f32)
    inverse_deviation = lax.rsqrt(lax.optimization_barrier(jnp.mean(hidden_state * hidden_state, axis=1, keepdims=True)) + EPS)
    norm_multiplier = final_norm_weight.astype(f32)
    standardized_state = hidden_state * inverse_deviation
    normalized_state = standardized_state * norm_multiplier
    grid = normalized_state.reshape(N_DP, seqs, SEQ_LEN, D)
    lengths = jnp.concatenate([query_lengths.reshape(N_DP, Q_DEV), passage_lengths.reshape(N_DP, P_DEV)], axis=1)
    slots = jnp.arange(SEQ_LEN, dtype=jnp.int32)
    valid = (slots[None, None, :] < lengths[:, :, None]).astype(f32)
    weights = valid / lengths[:, :, None].astype(f32)
    pooled = jnp.einsum('gst,gstd->gsd', weights, grid)
    norms = jnp.sqrt(lax.optimization_barrier(jnp.sum(pooled * pooled, axis=2, keepdims=True)) + EPS)
    unit = pooled / norms
    q_emb = unit[:, :Q_DEV].reshape(QUERIES, D).astype(jnp.bfloat16)
    p_emb = unit[:, Q_DEV:].reshape(PASSAGES, D).astype(jnp.bfloat16)
    logits = LOGIT_SCALE * jnp.dot(q_emb, p_emb.T, preferred_element_type=f32)
    columns = jnp.arange(PASSAGES, dtype=jnp.int32)
    is_pos = (columns[None, :] == positive_index[:, None]).astype(f32)
    query_tile = jnp.arange(QUERIES, dtype=jnp.int32) // TILE
    tile_rows = tile_mask[query_tile].astype(f32)
    allowed = jnp.broadcast_to(tile_rows[:, :, None], (QUERIES, P_TILES, TILE)).reshape(QUERIES, PASSAGES)
    keep = jnp.maximum(allowed, is_pos)
    expo = jnp.exp(logits) * keep
    denom = lax.optimization_barrier(jnp.sum(expo, axis=1))
    pos_logit = lax.optimization_barrier(jnp.sum(logits * is_pos, axis=1))
    query_loss = jnp.log(denom) - pos_logit
    dlogits = (LOSS_SCALE * (expo / denom[:, None] - is_pos)).astype(jnp.bfloat16)
    d_q = LOGIT_SCALE * jnp.dot(dlogits, p_emb, preferred_element_type=f32)
    d_p = LOGIT_SCALE * jnp.dot(dlogits.T, q_emb, preferred_element_type=f32)
    d_unit = jnp.concatenate([d_q.reshape(N_DP, Q_DEV, D), d_p.reshape(N_DP, P_DEV, D)], axis=1)
    inner = lax.optimization_barrier(jnp.sum(unit * d_unit, axis=2, keepdims=True))
    d_pooled = (d_unit - unit * inner) / norms
    normalized_output_gradient = (weights[:, :, :, None] * d_pooled[:, :, None, :]).reshape(TOKENS, D)
    standardized_gradient = normalized_output_gradient * norm_multiplier
    average_correction = lax.optimization_barrier(jnp.mean(standardized_gradient * standardized_state, axis=1, keepdims=True))
    residual_gradient = (inverse_deviation * (standardized_gradient - standardized_state * average_correction)).astype(jnp.bfloat16)
    group_width = D // N_TENSOR
    total = jnp.zeros((TOKENS, HW), f32)
    for group in range(N_TENSOR):
        left = residual_gradient[:, group * group_width:(group + 1) * group_width]
        right = out_weight[:, group * group_width:(group + 1) * group_width]
        piece = jnp.dot(left, right.T, preferred_element_type=f32).astype(jnp.bfloat16)
        total = total + lax.optimization_barrier(piece).astype(f32)
    d_context = total.astype(jnp.bfloat16)
    return (query_loss, residual_gradient, d_context)
```

```python
import jax
import jax.numpy as jnp
from jax import lax
from jax.sharding import Mesh
from jax.sharding import PartitionSpec as P

Q_DEV = 16
P_DEV = 16
SEQ_LEN = 16
TILE = 128
SEQS = Q_DEV + P_DEV

EPS = 1e-06
LOGIT_SCALE = 20.0
LOSS_SCALE = 1024.0

NZ, NX, NYH, NYL, NC = 8, 4, 2, 4, 2
NT = NYL * NC
T = ("yl", "core")
ROW = ("x",)
COL = ("z", "yh")
N_ROW = NX
N_COL = NZ * NYH


def exchange(parts, axes):
    return lax.all_to_all(parts, axes, 0, 0)


def gather(value, axes, count):
    return exchange(jnp.broadcast_to(value, (count,) + value.shape), axes)


def body(
    context,
    residual,
    out_weight,
    final_norm_weight,
    query_lengths,
    passage_lengths,
    positive_index,
    tile_mask,
):
    f32 = jnp.float32
    bf16 = jnp.bfloat16
    tokens, width = residual.shape
    hw_dev = context.shape[1]
    hw = out_weight.shape[0]
    full_width = width * NT
    core = lax.axis_index("core")
    gain = final_norm_weight

    positives = gather(jnp.broadcast_to(positive_index[None, :], (8, Q_DEV)), ROW, N_ROW)[:, 0, :]
    positives = positives.reshape(N_ROW, NT, Q_DEV // NT)
    rows_pos = lax.dynamic_index_in_dim(positives, lax.axis_index(T), 1, keepdims=False).reshape(-1)

    weight_by_core = out_weight.reshape(NYL, NC, hw_dev, width)
    own_half = lax.dynamic_index_in_dim(weight_by_core, core, 1, keepdims=False).reshape(-1, width)
    other_half = lax.dynamic_index_in_dim(weight_by_core, 1 - core, 1, keepdims=False).reshape(
        -1, width
    )
    own_context = lax.all_gather(context, "yl", axis=1, tiled=True)
    other_context = lax.ppermute(own_context, "core", [(0, 1), (1, 0)])
    hidden = residual.astype(f32) + jnp.dot(own_context, own_half, preferred_element_type=f32)
    hidden = hidden + jnp.dot(other_context, other_half, preferred_element_type=f32)

    squares = jnp.sum(hidden * hidden, axis=1).reshape(tokens // 128, 128)
    squares = jnp.sum(gather(squares, T, NT), axis=0).reshape(tokens)
    inv = lax.rsqrt(squares / full_width + EPS)

    lengths = jnp.concatenate([query_lengths, passage_lengths], axis=0)
    slots = jnp.arange(SEQ_LEN, dtype=jnp.int32)
    valid = (slots[None, :] < lengths[:, None]).astype(f32)
    weights = valid / lengths[:, None].astype(f32)
    scale = weights * inv.reshape(SEQS, SEQ_LEN)
    by_seq = hidden.reshape(SEQS, SEQ_LEN, width)
    pooled = jnp.sum(by_seq * scale[:, :, None], axis=1) * gain
    pooled_low = pooled.astype(bf16)
    pooled_gain = pooled * gain

    lifted = jnp.concatenate([hidden.astype(bf16), pooled_gain.astype(bf16)], axis=0)
    lifted = lax.dot_general(
        out_weight, lifted, (((1,), (1,)), ((), ())), preferred_element_type=f32
    ).astype(bf16)
    lifted = lax.psum_scatter(lifted, T, scatter_dimension=0, tiled=True)

    q_rows = gather(pooled_low[:Q_DEV], ROW, N_ROW)
    q_rows = q_rows.reshape(N_ROW, NT, Q_DEV // NT, width).swapaxes(0, 1).reshape(-1, width)
    p_cols = gather(pooled_low[Q_DEV:], COL, N_COL).reshape(-1, width)
    n_rows, n_cols = q_rows.shape[0], p_cols.shape[0]
    share = n_rows // NT
    scores = lax.dot_general(
        q_rows, p_cols, (((1,), (1,)), ((), ())), preferred_element_type=f32
    ).reshape(NT, share, n_cols)
    q_wide, p_wide = q_rows.astype(f32), p_cols.astype(f32)
    q_sq = jnp.sum(q_wide * q_wide, axis=1).reshape(NT, share)
    p_sq = jnp.sum(p_wide * p_wide, axis=1)
    own_sq = jnp.sum(pooled * pooled, axis=1)
    cross = jnp.sum(by_seq * pooled_gain[:, None, :], axis=2).reshape(-1)
    common = jnp.concatenate([p_sq, own_sq, cross])
    side = jnp.concatenate([q_sq, jnp.broadcast_to(common, (NT,) + common.shape)], axis=1)
    side_width = -(-side.shape[1] // (share * 128)) * 128
    side = jnp.pad(side, ((0, 0), (0, share * side_width - side.shape[1])))
    payload = jnp.concatenate([scores, side.reshape(NT, share, side_width)], axis=2)
    summed = jnp.sum(exchange(payload, T), axis=0)
    scores = summed[:, :n_cols]
    side = summed[:, n_cols:].reshape(-1)
    q_sq = side[:share]
    p_sq = side[share : share + n_cols]
    own_sq = side[share + n_cols : share + n_cols + SEQS] + EPS
    cross = side[share + n_cols + SEQS : share + n_cols + SEQS + tokens]
    q_rn = lax.rsqrt(q_sq + EPS)[:, None]
    p_rn = lax.rsqrt(p_sq + EPS)[None, :]
    rn = q_rn * p_rn
    logits = LOGIT_SCALE * scores * rn

    z, x, yh = lax.axis_index("z"), lax.axis_index("x"), lax.axis_index("yh")
    col = jnp.arange(n_cols, dtype=jnp.int32)
    col_z, col_yh, col_in = col // (NYH * P_DEV), (col // P_DEV) % NYH, col % P_DEV
    passage = ((col_z * NX + x) * NYH + col_yh) * P_DEV + col_in
    row = jnp.arange(share, dtype=jnp.int32) // (Q_DEV // NT)
    query_tile = ((z * NX + row) * NYH + yh) * Q_DEV // TILE
    q_hot = (query_tile[:, None] == jnp.arange(tile_mask.shape[0])[None, :]).astype(f32)
    p_hot = ((passage // TILE)[None, :] == jnp.arange(tile_mask.shape[1])[:, None]).astype(f32)
    by_q = jnp.sum(q_hot[:, :, None] * tile_mask.astype(f32)[None, :, :], axis=1)
    allowed = jnp.sum(by_q[:, :, None] * p_hot[None, :, :], axis=1)
    is_pos = (passage[None, :] == rows_pos[:, None]).astype(f32)
    keep = jnp.maximum(allowed, is_pos)
    expo = jnp.exp(logits) * keep

    lane = jnp.arange(128, dtype=jnp.int32)[None, :]
    sums = jnp.where(
        lane == 0,
        jnp.sum(expo, axis=1)[:, None],
        jnp.where(lane == 1, jnp.sum(logits * is_pos, axis=1)[:, None], 0.0),
    )
    sums = jnp.sum(gather(sums, ROW, N_ROW), axis=0)
    denom = sums[:, :1]
    losses = (jnp.log(denom) - sums[:, 1:2]).reshape(N_ROW, Q_DEV // NT)
    query_loss = lax.dynamic_index_in_dim(losses, x, 0, keepdims=False)

    dlogits = (LOSS_SCALE * rn * (expo / denom - is_pos)).astype(bf16)
    dlogits = gather(dlogits, T, NT).reshape(n_rows, n_cols)
    d_q = jnp.dot(dlogits, p_cols, preferred_element_type=f32).astype(bf16)
    d_q = d_q.reshape(NT, N_ROW, Q_DEV // NT, width).swapaxes(0, 1).reshape(N_ROW, Q_DEV, width)
    d_p = lax.dot_general(
        dlogits, q_rows, (((0,), (0,)), ((), ())), preferred_element_type=f32
    ).astype(bf16)
    d_q = jnp.sum(exchange(d_q, ROW).astype(f32), axis=0)
    d_p = jnp.sum(exchange(d_p.reshape(N_COL, P_DEV, width), COL).astype(f32), axis=0)
    back = jnp.concatenate([d_q, d_p], axis=0)

    inner = jnp.sum(pooled * back, axis=1)
    back_gain = back * gain
    cross_back = jnp.sum(by_seq * back_gain[:, None, :], axis=2).reshape(-1)
    back_up = lax.dot_general(
        back_gain.astype(bf16), out_weight, (((1,), (1,)), ((), ())), preferred_element_type=f32
    )
    back_up = back_up.reshape(SEQS, NT, hw_dev).swapaxes(0, 1)
    side = jnp.concatenate([cross_back, inner])
    side_rows = -(-side.shape[0] // (8 * hw_dev)) * 8
    side = jnp.pad(side, (0, side_rows * hw_dev - side.shape[0])).reshape(1, side_rows, hw_dev)
    payload = jnp.concatenate([back_up, jnp.broadcast_to(side, (NT,) + side.shape[1:])], axis=1)
    summed = jnp.sum(exchange(payload, T), axis=0)
    back_up = summed[:SEQS]
    side = summed[SEQS:].reshape(-1)
    cross_back, inner = side[:tokens], side[tokens : tokens + SEQS]

    ratio = inner / own_sq
    lead = LOGIT_SCALE * scale
    mean = (
        lead
        * (cross_back.reshape(SEQS, SEQ_LEN) - ratio[:, None] * cross.reshape(SEQS, SEQ_LEN))
        / full_width
    )
    inv_seq = inv.reshape(SEQS, SEQ_LEN)
    trail = inv_seq * inv_seq * mean
    d_pooled = back_gain - ratio[:, None] * pooled_gain
    residual_gradient = (
        (lead[:, :, None] * d_pooled[:, None, :] - trail[:, :, None] * by_seq)
        .astype(bf16)
        .reshape(tokens, width)
    )
    lifted = lifted.T.astype(f32)
    seq_up = back_up - ratio[:, None] * lifted[tokens:]
    d_context = (
        (
            lead[:, :, None] * seq_up[:, None, :]
            - trail[:, :, None] * lifted[:tokens].reshape(SEQS, SEQ_LEN, hw_dev)
        )
        .astype(bf16)
        .reshape(tokens, hw_dev)
    )
    return (query_loss, residual_gradient, d_context)


def solution(mesh):
    fine = Mesh(
        mesh.devices.reshape(NZ, NX, NYH, NYL, NC), ("z", "x", "yh", "yl", "core")
    )
    dp = ("z", "x", "yh")
    in_specs = (
        P(dp, T),
        P(dp, T),
        P(None, T),
        P(T),
        P(dp),
        P(dp),
        P(dp),
        P(),
    )
    out_specs = (P(dp + T), P(dp, T), P(dp, T))
    return jax.shard_map(body, mesh=fine, in_specs=in_specs, out_specs=out_specs, check_vma=False)
```

```python
import jax
import jax.numpy as jnp
from jax import lax
from jax.sharding import Mesh
from jax.sharding import PartitionSpec as P

Q_DEV = 16
P_DEV = 16
SEQ_LEN = 16
TILE = 128
SEQS = Q_DEV + P_DEV

EPS = 1e-06
LOGIT_SCALE = 20.0
LOSS_SCALE = 1024.0

NZ, NX, NYH, NYL, NC = 8, 4, 2, 4, 2
NT = NYL * NC
T = ("yl", "core")
ROW = ("x",)
COL = ("z", "yh")
N_ROW = NX
N_COL = NZ * NYH


def exchange(parts, axes):
    return lax.all_to_all(parts, axes, 0, 0)


def gather(value, axes, count):
    return exchange(jnp.broadcast_to(value, (count,) + value.shape), axes)


def body(
    context,
    residual,
    out_weight,
    final_norm_weight,
    query_lengths,
    passage_lengths,
    positive_index,
    tile_mask,
):
    f32 = jnp.float32
    bf16 = jnp.bfloat16
    tokens, width = residual.shape
    hw_dev = context.shape[1]
    hw = out_weight.shape[0]
    full_width = width * NT
    core = lax.axis_index("core")
    gain = final_norm_weight

    weight_by_core = out_weight.reshape(NYL, NC, hw_dev, width)
    own_half = lax.dynamic_index_in_dim(weight_by_core, core, 1, keepdims=False).reshape(-1, width)
    other_half = lax.dynamic_index_in_dim(weight_by_core, 1 - core, 1, keepdims=False).reshape(
        -1, width
    )
    halves = []
    step = tokens // 2
    for first in (0, step):
        part = lax.slice_in_dim(context, first, first + step, axis=0)
        own_context = lax.all_gather(part, "yl", axis=1, tiled=True)
        other_context = lax.ppermute(own_context, "core", [(0, 1), (1, 0)])
        half = jnp.dot(own_context, own_half, preferred_element_type=f32)
        halves.append(half + jnp.dot(other_context, other_half, preferred_element_type=f32))
    hidden = residual.astype(f32) + jnp.concatenate(halves, axis=0)

    squares = jnp.sum(hidden * hidden, axis=1).reshape(tokens // 128, 128)
    squares = jnp.sum(gather(squares, T, NT), axis=0).reshape(tokens)
    inv = lax.rsqrt(squares / full_width + EPS)

    lengths = jnp.concatenate([query_lengths, passage_lengths], axis=0)
    slots = jnp.arange(SEQ_LEN, dtype=jnp.int32)
    valid = (slots[None, :] < lengths[:, None]).astype(f32)
    weights = valid / lengths[:, None].astype(f32)
    scale = weights * inv.reshape(SEQS, SEQ_LEN)
    by_seq = hidden.reshape(SEQS, SEQ_LEN, width)
    pooled = jnp.sum(by_seq * scale[:, :, None], axis=1) * gain
    pooled_low = pooled.astype(bf16)
    pooled_gain = pooled * gain

    lifted = jnp.concatenate([hidden.astype(bf16), pooled_gain.astype(bf16)], axis=0)
    lifted = lax.dot_general(
        out_weight, lifted, (((1,), (1,)), ((), ())), preferred_element_type=f32
    ).astype(bf16)
    pooled_low, lifted = lax.optimization_barrier((pooled_low, lifted))
    lifted = lax.psum_scatter(lifted, T, scatter_dimension=0, tiled=True)

    position = jnp.stack([positive_index // 32, positive_index % 32], axis=1).astype(bf16)
    position = jnp.pad(position, ((0, 0), (0, 126)))
    q_rows = gather(jnp.concatenate([pooled_low[:Q_DEV], position], axis=1), ROW, N_ROW)
    q_rows = q_rows.reshape(N_ROW, NT, Q_DEV // NT, -1).swapaxes(0, 1).reshape(N_ROW * Q_DEV, -1)
    position = q_rows[:, width : width + 2].astype(jnp.int32)
    position = position[:, 0] * 32 + position[:, 1]
    q_rows = q_rows[:, :width]
    p_cols = gather(pooled_low[Q_DEV:], COL, N_COL).reshape(-1, width)
    n_rows, n_cols = q_rows.shape[0], p_cols.shape[0]
    share = n_rows // NT
    scores = lax.dot_general(
        q_rows, p_cols, (((1,), (1,)), ((), ())), preferred_element_type=f32
    ).reshape(NT, share, n_cols)
    q_wide, p_wide = q_rows.astype(f32), p_cols.astype(f32)
    q_sq = jnp.sum(q_wide * q_wide, axis=1).reshape(NT, share)
    p_sq = jnp.sum(p_wide * p_wide, axis=1)
    own_sq = jnp.sum(pooled * pooled, axis=1)
    cross = jnp.sum(by_seq * pooled_gain[:, None, :], axis=2).reshape(-1)
    common = jnp.concatenate([p_sq, own_sq, cross])
    side = jnp.concatenate([q_sq, jnp.broadcast_to(common, (NT,) + common.shape)], axis=1)
    side_width = -(-side.shape[1] // (share * 128)) * 128
    side = jnp.pad(side, ((0, 0), (0, share * side_width - side.shape[1])))
    payload = jnp.concatenate([scores, side.reshape(NT, share, side_width)], axis=2)
    summed = jnp.sum(exchange(payload, T), axis=0)
    scores = summed[:, :n_cols]
    side = summed[:, n_cols:].reshape(-1)
    q_sq = side[:share]
    p_sq = side[share : share + n_cols]
    own_sq = side[share + n_cols : share + n_cols + SEQS] + EPS
    cross = side[share + n_cols + SEQS : share + n_cols + SEQS + tokens]
    q_rn = lax.rsqrt(q_sq + EPS)[:, None]
    p_rn = lax.rsqrt(p_sq + EPS)[None, :]
    rn = q_rn * p_rn
    logits = LOGIT_SCALE * scores * rn

    z, x, yh = lax.axis_index("z"), lax.axis_index("x"), lax.axis_index("yh")
    col = jnp.arange(n_cols, dtype=jnp.int32)
    col_z, col_yh, col_in = col // (NYH * P_DEV), (col // P_DEV) % NYH, col % P_DEV
    passage = ((col_z * NX + x) * NYH + col_yh) * P_DEV + col_in
    row = jnp.arange(share, dtype=jnp.int32) // (Q_DEV // NT)
    query_tile = ((z * NX + row) * NYH + yh) * Q_DEV // TILE
    q_hot = (query_tile[:, None] == jnp.arange(tile_mask.shape[0])[None, :]).astype(f32)
    p_hot = ((passage // TILE)[None, :] == jnp.arange(tile_mask.shape[1])[:, None]).astype(f32)
    by_q = jnp.sum(q_hot[:, :, None] * tile_mask.astype(f32)[None, :, :], axis=1)
    allowed = jnp.sum(by_q[:, :, None] * p_hot[None, :, :], axis=1)
    me = lax.axis_index(T)
    at_pos = (passage[None, :] == position[:, None]).astype(f32)
    is_pos = lax.dynamic_slice_in_dim(at_pos, me * share, share, axis=0)
    others = jnp.exp(logits) * allowed * (1.0 - is_pos)

    sums = jnp.stack(
        [
            jnp.sum(others, axis=1),
            jnp.sum(jnp.exp(logits) * is_pos, axis=1),
            jnp.sum(logits * is_pos, axis=1),
        ],
        axis=1,
    )
    high = lax.reduce_precision(sums, 8, 7)
    middle = lax.reduce_precision(sums - high, 8, 7)
    low = sums - high - middle
    sums = jnp.pad(jnp.concatenate([high, middle, low], axis=1), ((0, 0), (0, 128 - 9)))
    terms = rn * (others + is_pos)
    payload = jnp.concatenate([terms.astype(bf16), sums.astype(bf16)], axis=1)
    payload = gather(payload, ROW + T, N_ROW * NT).reshape(N_ROW, NT * share, n_cols + 128)
    sums = payload[:, :, n_cols : n_cols + 9].astype(f32)
    sums = jnp.sum(sums.reshape(N_ROW, NT * share, 3, 3), axis=(0, 2))
    denom = sums[:, 0] + sums[:, 1]
    losses = (jnp.log(denom) - sums[:, 2]).reshape(NT, N_ROW, Q_DEV // NT)
    query_loss = lax.dynamic_slice(losses, (me, x, 0), (1, 1, Q_DEV // NT)).reshape(-1)
    terms = lax.dynamic_index_in_dim(payload, x, 0, keepdims=False)[:, :n_cols].astype(f32)
    other_factor = LOSS_SCALE / denom
    pos_factor = -other_factor * sums[:, 0]
    factor = other_factor[:, None] + at_pos * (pos_factor - other_factor)[:, None]
    dlogits = (terms * factor).astype(bf16)
    d_q = jnp.dot(dlogits, p_cols, preferred_element_type=f32).astype(bf16)
    d_q = d_q.reshape(NT, N_ROW, Q_DEV // NT, width).swapaxes(0, 1).reshape(N_ROW, Q_DEV, width)
    d_p = lax.dot_general(
        dlogits, q_rows, (((0,), (0,)), ((), ())), preferred_element_type=f32
    ).astype(bf16)
    d_q = jnp.sum(exchange(d_q, ROW).astype(f32), axis=0)
    d_p, lifted = lax.optimization_barrier((d_p, lifted))
    d_p = jnp.sum(exchange(d_p.reshape(N_COL, P_DEV, width), COL).astype(f32), axis=0)
    back = jnp.concatenate([d_q, d_p], axis=0)

    inner = jnp.sum(pooled * back, axis=1)
    back_gain = back * gain
    cross_back = jnp.sum(by_seq * back_gain[:, None, :], axis=2).reshape(-1)
    back_up = lax.dot_general(
        back_gain.astype(bf16), out_weight, (((1,), (1,)), ((), ())), preferred_element_type=f32
    )
    back_up = back_up.reshape(SEQS, NT, hw_dev).swapaxes(0, 1)
    side = jnp.pad(jnp.concatenate([cross_back, inner]), (0, 8 * hw_dev - tokens - SEQS))
    high = lax.reduce_precision(side, 8, 7)
    side = jnp.concatenate([high, side - high]).astype(bf16).reshape(1, 16, hw_dev)
    payload = jnp.concatenate(
        [back_up.astype(bf16), jnp.broadcast_to(side, (NT,) + side.shape[1:])], axis=1
    )
    summed = jnp.sum(exchange(payload, T).astype(f32), axis=0)
    back_up = summed[:SEQS]
    side = (summed[SEQS : SEQS + 8] + summed[SEQS + 8 :]).reshape(-1)
    cross_back, inner = side[:tokens], side[tokens : tokens + SEQS]

    ratio = inner / own_sq
    lead = LOGIT_SCALE * scale
    mean = (
        lead
        * (cross_back.reshape(SEQS, SEQ_LEN) - ratio[:, None] * cross.reshape(SEQS, SEQ_LEN))
        / full_width
    )
    inv_seq = inv.reshape(SEQS, SEQ_LEN)
    trail = inv_seq * inv_seq * mean
    d_pooled = back_gain - ratio[:, None] * pooled_gain
    residual_gradient = (
        (lead[:, :, None] * d_pooled[:, None, :] - trail[:, :, None] * by_seq)
        .astype(bf16)
        .reshape(tokens, width)
    )
    lifted = lifted.T.astype(f32)
    seq_up = back_up - ratio[:, None] * lifted[tokens:]
    d_context = (
        (
            lead[:, :, None] * seq_up[:, None, :]
            - trail[:, :, None] * lifted[:tokens].reshape(SEQS, SEQ_LEN, hw_dev)
        )
        .astype(bf16)
        .reshape(tokens, hw_dev)
    )
    return (query_loss, residual_gradient, d_context)


def solution(mesh):
    fine = Mesh(
        mesh.devices.reshape(NZ, NX, NYH, NYL, NC), ("z", "x", "yh", "yl", "core")
    )
    dp = ("z", "x", "yh")
    in_specs = (
        P(dp, T),
        P(dp, T),
        P(None, T),
        P(T),
        P(dp),
        P(dp),
        P(dp),
        P(),
    )
    out_specs = (P(dp + T), P(dp, T), P(dp, T))
    return jax.shard_map(body, mesh=fine, in_specs=in_specs, out_specs=out_specs, check_vma=False)
```

```python
import functools

import jax
import jax.numpy as jnp
from jax import lax
from jax.experimental import pallas as pl
from jax.experimental.pallas import tpu as pltpu
from jax.sharding import Mesh
from jax.sharding import PartitionSpec as P

Q_DEV = 16
P_DEV = 16
SEQ_LEN = 16
SEQS = Q_DEV + P_DEV
TOKENS = SEQS * SEQ_LEN
HALF = TOKENS // 2

EPS = 1e-06
LOGIT_SCALE = 20.0
LOSS_SCALE = 1024.0

NZ, NX, NYH, NYL, NC = 8, 4, 2, 4, 2
NT = NYL * NC
T = ("yl", "core")
ROW = ("x",)
COL = ("z", "yh")
N_ROW = NX
N_COL = NZ * NYH
ROWS = N_ROW * Q_DEV
COLS = N_COL * P_DEV
SHARE = ROWS // NT
PAIR = Q_DEV // NT
HW_DEV = 256
WIDTH = 512
FULL = WIDTH * NT

f32 = jnp.float32
bf16 = jnp.bfloat16
i32 = jnp.int32


def dot(a, b, dims=((1,), (0,)), exact=False):
    return lax.dot_general(
        a,
        b,
        (dims, ((), ())),
        preferred_element_type=f32,
        precision=lax.Precision.HIGHEST if exact else None,
    )


def iota(shape, dim):
    return lax.broadcasted_iota(i32, shape, dim)


def to_col(row, n):
    eye = iota((n, n), 0) == iota((n, n), 1)
    return jnp.sum(jnp.where(eye, row, 0.0), axis=1, keepdims=True)


def to_row(col, n):
    eye = iota((n, n), 0) == iota((n, n), 1)
    return jnp.sum(jnp.where(eye, col, 0.0), axis=0, keepdims=True)


def seg_mask():
    return iota((SEQS, TOKENS), 1) // SEQ_LEN == iota((SEQS, TOKENS), 0)


def split(value):
    high = value.astype(bf16).astype(f32)
    return high, value - high


def row_order():
    shape = (ROWS, ROWS)
    here, there = iota(shape, 0), iota(shape, 1)
    k, x, j = here // SHARE, (here % SHARE) // PAIR, here % PAIR
    return (there == x * Q_DEV + k * PAIR + j).astype(f32).astype(bf16)


def hidden_kernel(last, ids, own, other, weight, residual, *refs):
    if last:
        before, hidden, low, payload = refs
    else:
        hidden, low, payload = refs
    core = ids[0]
    total = residual[...].astype(f32)
    for y in range(NYL):
        part = slice(y * HW_DEV, (y + 1) * HW_DEV)
        for ref, c in ((own, core), (other, 1 - core)):
            first = pl.multiple_of((y * NC + c) * HW_DEV, HW_DEV)
            total = total + dot(ref[:, part], weight[pl.ds(first, HW_DEV), :])
    hidden[...] = total
    low[...] = total.astype(bf16)
    square = jnp.sum(total * total, axis=1, keepdims=True)
    rows = [to_row(square[b * 128 : (b + 1) * 128], 128) for b in range(HALF // 128)]
    if last:
        rows = [before[0:1], before[1:2]] + rows + [jnp.zeros((4, 128), f32)]
        payload[...] = jnp.broadcast_to(jnp.concatenate(rows, axis=0)[None], (NT, 8, 128))
    else:
        payload[...] = jnp.concatenate(rows + [jnp.zeros((6, 128), f32)], axis=0)


def pool_kernel(
    squares, q_len, p_len, position, gain, hidden_a, hidden_b, wi, inv, pooled, lift, q_pay, p_pay
):
    total = jnp.sum(squares[...], axis=0)
    total = jnp.concatenate([total[b : b + 1] for b in range(TOKENS // 128)], axis=1)
    inverse = lax.rsqrt(total / FULL + EPS)
    inv[...] = inverse
    lengths = jnp.concatenate(
        [to_col(q_len[...].astype(f32), Q_DEV), to_col(p_len[...].astype(f32), P_DEV)], axis=0
    )
    slot = (iota((SEQS, TOKENS), 1) % SEQ_LEN).astype(f32)
    weight = jnp.where(seg_mask() & (slot < lengths), 1.0 / lengths, 0.0) * inverse
    wi[...] = weight
    value = dot(weight[:, :HALF], hidden_a[...], exact=True)
    value = value + dot(weight[:, HALF:], hidden_b[...], exact=True)
    value = value * gain[...]
    pooled[...] = value
    lift[...] = (value * gain[...]).astype(bf16)
    low = value.astype(bf16)
    where = to_col(position[...].astype(f32), Q_DEV)
    high = jnp.floor(where * (1.0 / 32.0))
    lane = iota((Q_DEV, 128), 1)
    where = jnp.where(lane == 0, high, jnp.where(lane == 1, where - 32.0 * high, 0.0))
    q_pay[:, :, :WIDTH] = jnp.broadcast_to(low[None, :Q_DEV], (N_ROW, Q_DEV, WIDTH))
    q_pay[:, :, WIDTH:] = jnp.broadcast_to(where.astype(bf16)[None], (N_ROW, Q_DEV, 128))
    p_pay[...] = jnp.broadcast_to(low[None, Q_DEV:], (N_COL, P_DEV, WIDTH))


def lift_kernel(low_a, low_b, pooled, weight, out):
    for n in range(NT):
        part = slice(n * HW_DEV, (n + 1) * HW_DEV)
        w = weight[part, :]
        out[:HALF, part] = dot(low_a[...], w, ((1,), (1,))).astype(bf16)
        out[HALF:TOKENS, part] = dot(low_b[...], w, ((1,), (1,))).astype(bf16)
        out[TOKENS:, part] = dot(pooled[...], w, ((1,), (1,))).astype(bf16)


def score_kernel(q_all, p_all, pooled, lift, low_a, low_b, payload, position):
    order = row_order()
    q_rows = dot(order, q_all[...].reshape(ROWS, WIDTH + 128))
    position[...] = q_rows[:, WIDTH:]
    q_rows = q_rows[:, :WIDTH]
    p_cols = p_all[...].reshape(COLS, WIDTH)
    scores = dot(q_rows.astype(bf16), p_cols, ((1,), (1,)))
    payload[:, :, :COLS] = scores.reshape(NT, SHARE, COLS)
    q_sq = to_row(jnp.sum(q_rows * q_rows, axis=1, keepdims=True), ROWS)
    p_wide = p_cols.astype(f32)
    p_sq = jnp.sum(p_wide * p_wide, axis=1, keepdims=True)
    own = pooled[...]
    own_sq = to_row(jnp.sum(own * own, axis=1, keepdims=True), SEQS)
    cross = [dot(lift[...], low[...], ((1,), (1,))) for low in (low_a, low_b)]
    cross = jnp.sum(jnp.where(seg_mask(), jnp.concatenate(cross, axis=1), 0.0), axis=0, keepdims=True)
    rows = [to_row(p_sq[b * 128 : (b + 1) * 128], 128) for b in range(COLS // 128)]
    rows += [cross[:, b * 128 : (b + 1) * 128] for b in range(TOKENS // 128)]
    rows.append(jnp.concatenate([own_sq, jnp.zeros((1, 128 - SEQS), f32)], axis=1))
    rows.append(jnp.concatenate([q_sq, jnp.zeros((1, 128 - ROWS), f32)], axis=1))
    payload[:, :, COLS:] = jnp.broadcast_to(jnp.concatenate(rows, axis=0)[None], (NT, 8, 128))


def at_positive(position, x):
    where = position[:, 0:1] * 32.0 + position[:, 1:2]
    col = iota((position.shape[0], COLS), 1)
    passage = (col // 32) * 128 + x * 32 + col % 32
    return passage.astype(f32) == where


def softmax_kernel(ids, tile_mask, parts, position, payload, side):
    me, z, x = ids[1], ids[2], ids[3]
    total = jnp.sum(parts[...], axis=0)
    side[...] = total[:, COLS:]
    block = total[:, COLS:]
    scores = total[:, :COLS]
    p_sq = jnp.concatenate([block[0:1], block[1:2]], axis=1)
    own = iota((SHARE, 128), 1) == me * SHARE + iota((SHARE, 128), 0)
    q_sq = jnp.sum(jnp.where(own, block[7:8], 0.0), axis=1, keepdims=True)
    rn = lax.rsqrt(q_sq + EPS) * lax.rsqrt(p_sq + EPS)
    logits = LOGIT_SCALE * scores * rn
    block_of = iota((SHARE, COLS), 1) // 32
    allowed = jnp.zeros((SHARE, COLS), f32)
    for j in range(NZ):
        allowed = jnp.where(block_of == j, tile_mask[z, j].astype(f32), allowed)
    first = pl.multiple_of(me * SHARE, SHARE)
    is_pos = at_positive(position[pl.ds(first, SHARE), :], x)
    expo = jnp.exp(logits)
    others = jnp.where(is_pos, 0.0, expo * allowed)
    sums = [
        jnp.sum(others, axis=1, keepdims=True),
        jnp.sum(jnp.where(is_pos, expo, 0.0), axis=1, keepdims=True),
        jnp.sum(jnp.where(is_pos, logits, 0.0), axis=1, keepdims=True),
    ]
    lane = iota((SHARE, COLS), 1)
    row = jnp.zeros((SHARE, COLS), f32)
    for i, value in enumerate(sums):
        high, rest = split(value)
        middle, low = split(rest)
        for j, piece in enumerate((high, middle, low)):
            row = jnp.where(lane == 3 * i + j, piece, row)
    terms = rn * jnp.where(is_pos, 1.0, others)
    payload[...] = jnp.broadcast_to(
        jnp.concatenate([terms, row], axis=0).astype(bf16)[None], payload.shape
    )


def back_kernel(ids, parts, position, q_all, p_all, loss, q_pay, p_pay):
    me, x = ids[1], ids[3]
    total = jnp.zeros((NT, SHARE, 128), f32)
    for k in range(N_ROW):
        total = total + parts[k * NT : (k + 1) * NT, :, :128].astype(f32)[:, SHARE:, :]
    total = total.reshape(ROWS, 128)
    lane = iota((ROWS, 128), 1)
    others, positive, logit = (
        jnp.sum(jnp.where(lane // 3 == i, total, 0.0), axis=1, keepdims=True) for i in range(3)
    )
    denom = others + positive
    losses = jnp.log(denom) - logit
    row = me * SHARE + x * PAIR + iota((ROWS, 128), 1)
    mine = (iota((ROWS, 128), 0) == row) & (lane < PAIR)
    loss[...] = jnp.broadcast_to(
        jnp.sum(jnp.where(mine, losses, 0.0), axis=0, keepdims=True), loss.shape
    )
    first = pl.multiple_of(x * NT, NT)
    terms = parts[pl.ds(first, NT)].astype(f32)[:, :SHARE, :].reshape(ROWS, COLS)
    factor = LOSS_SCALE / denom
    terms = terms * jnp.where(at_positive(position[...], x), -factor * others, factor)
    terms = dot(row_order(), terms.astype(bf16), ((0,), (0,))).astype(bf16)
    d_q = dot(terms, p_all[...].reshape(COLS, WIDTH))
    q_pay[...] = d_q.astype(bf16).reshape(N_ROW, Q_DEV, WIDTH)
    d_p = dot(terms, q_all[...].reshape(ROWS, WIDTH + 128)[:, :WIDTH], ((0,), (0,)))
    p_pay[...] = d_p.astype(bf16).reshape(N_COL, P_DEV, WIDTH)


def up_kernel(q_parts, p_parts, pooled, gain, low_a, low_b, weight, back_gain, payload):
    back = jnp.concatenate(
        [jnp.sum(q_parts[...].astype(f32), axis=0), jnp.sum(p_parts[...].astype(f32), axis=0)],
        axis=0,
    )
    inner = to_row(jnp.sum(pooled[...] * back, axis=1, keepdims=True), SEQS)
    scaled = back * gain[...]
    back_gain[...] = scaled
    scaled = scaled.astype(bf16)
    cross = [dot(scaled, low[...], ((1,), (1,))) for low in (low_a, low_b)]
    cross = jnp.sum(jnp.where(seg_mask(), jnp.concatenate(cross, axis=1), 0.0), axis=0, keepdims=True)
    inner = jnp.concatenate([inner, jnp.zeros((1, HW_DEV - SEQS), f32)], axis=1)
    rows = jnp.concatenate([cross[:, :HW_DEV], cross[:, HW_DEV:], inner, jnp.zeros((5, HW_DEV), f32)], axis=0)
    high, low = split(rows)
    side = jnp.concatenate([high, low], axis=0).astype(bf16)
    for n in range(NT):
        w = weight[n * HW_DEV : (n + 1) * HW_DEV, :]
        payload[n, :SEQS, :] = dot(scaled, w, ((1,), (1,))).astype(bf16)
        payload[n, SEQS:, :] = side


def final_kernel(parts, side, wi, inv, pooled, gain, back_gain, hidden_a, hidden_b, lifted, d_res, d_ctx):
    total = jnp.sum(parts[...].astype(f32), axis=0)
    rows = total[SEQS : SEQS + 8] + total[SEQS + 8 :]
    cross_back = jnp.concatenate([rows[0:1], rows[1:2]], axis=1)
    inner = rows[2:3, :SEQS]
    block = side[...]
    cross = jnp.concatenate([block[b : b + 1] for b in range(2, 6)], axis=1)
    ratio = to_col(inner / (block[6:7, :SEQS] + EPS), SEQS)
    lead = LOGIT_SCALE * wi[...]
    inverse = inv[...]
    by_token = jnp.sum(lead * (cross_back - ratio * cross), axis=0, keepdims=True)
    trail = inverse * inverse * by_token / FULL
    d_pooled = back_gain[...] - ratio * (pooled[...] * gain[...])
    seq_up = total[:SEQS] - ratio * lifted[TOKENS:, :].astype(f32)
    both = jnp.concatenate([d_pooled, seq_up], axis=1)
    for b in range(TOKENS // 128):
        part = slice(b * 128, (b + 1) * 128)
        hidden = (hidden_a, hidden_b)[b * 128 // HALF]
        inner_part = slice(b * 128 % HALF, b * 128 % HALF + 128)
        spread = dot(lead[:, part], both, ((0,), (0,)), exact=True)
        column = to_col(trail[:, part], 128)
        d_res[part, :] = (spread[:, :WIDTH] - column * hidden[inner_part, :]).astype(bf16)
        d_ctx[part, :] = (spread[:, WIDTH:] - column * lifted[part, :].astype(f32)).astype(bf16)


VMEM = pl.BlockSpec(memory_space=pltpu.VMEM)
SMEM = pl.BlockSpec(memory_space=pltpu.SMEM)


def call(kernel, name, outs, args, scalars=0, flops=1 << 20):
    out = [jax.ShapeDtypeStruct(shape, dtype) for shape, dtype in outs]
    size = sum(a.size * a.dtype.itemsize for a in (*args, *out))
    return pl.pallas_call(
        kernel,
        out_shape=out,
        in_specs=[SMEM] * scalars + [VMEM] * (len(args) - scalars),
        out_specs=[VMEM] * len(out),
        compiler_params=pltpu.CompilerParams(vmem_limit_bytes=40 << 20),
        cost_estimate=pl.CostEstimate(flops=flops, bytes_accessed=size, transcendentals=0),
        name=name,
    )(*args)


def exchange(parts, axes):
    return lax.all_to_all(parts, axes, 0, 0)


def body(
    context,
    residual,
    out_weight,
    final_norm_weight,
    query_lengths,
    passage_lengths,
    positive_index,
    tile_mask,
):
    me = lax.axis_index(T)
    ids = jnp.stack(
        [lax.axis_index("core"), me, lax.axis_index("z"), lax.axis_index("x")]
    ).astype(i32)
    gain = final_norm_weight.reshape(1, WIDTH)

    parts = []
    for first in (0, HALF):
        own = lax.all_gather(context[first : first + HALF], "yl", axis=1, tiled=True)
        parts.append((own, lax.ppermute(own, "core", [(0, 1), (1, 0)])))
    hidden_outs = [((HALF, WIDTH), f32), ((HALF, WIDTH), bf16)]
    hidden_a, low_a, squares = call(
        functools.partial(hidden_kernel, False),
        "hidden_a",
        hidden_outs + [((8, 128), f32)],
        (ids, *parts[0], out_weight, residual[:HALF]),
        1,
        flops=2 * HALF * 2048 * WIDTH,
    )
    hidden_b, low_b, squares = call(
        functools.partial(hidden_kernel, True),
        "hidden_b",
        hidden_outs + [((NT, 8, 128), f32)],
        (ids, *parts[1], out_weight, residual[HALF:], squares),
        1,
        flops=2 * HALF * 2048 * WIDTH,
    )
    squares = exchange(squares, T)

    wi, inv, pooled, lift, q_pay, p_pay = call(
        pool_kernel,
        "pool",
        [
            ((SEQS, TOKENS), f32),
            ((1, TOKENS), f32),
            ((SEQS, WIDTH), f32),
            ((SEQS, WIDTH), bf16),
            ((N_ROW, Q_DEV, WIDTH + 128), bf16),
            ((N_COL, P_DEV, WIDTH), bf16),
        ],
        (
            squares,
            query_lengths.reshape(1, Q_DEV),
            passage_lengths.reshape(1, P_DEV),
            positive_index.reshape(1, Q_DEV),
            gain,
            hidden_a,
            hidden_b,
        ),
    )
    q_all = exchange(q_pay, ROW)
    (lifted,) = call(
        lift_kernel,
        "lift",
        [((TOKENS + SEQS, NT * HW_DEV), bf16)],
        (low_a, low_b, lift, out_weight),
        flops=2 * TOKENS * 2048 * WIDTH,
    )
    p_pay, lifted = lax.optimization_barrier((p_pay, lifted))
    lifted = lax.psum_scatter(lifted, T, scatter_dimension=1, tiled=True)
    p_all = exchange(p_pay, COL)

    payload, position = call(
        score_kernel,
        "score",
        [((NT, SHARE, COLS + 128), f32), ((ROWS, 128), f32)],
        (q_all, p_all, pooled, lift, low_a, low_b),
    )
    payload, side = call(
        softmax_kernel,
        "softmax",
        [((N_ROW * NT, 2 * SHARE, COLS), bf16), ((SHARE, 128), f32)],
        (ids, tile_mask, exchange(payload, T), position),
        2,
    )
    loss, q_pay, p_pay = call(
        back_kernel,
        "back",
        [((8, 128), f32), ((N_ROW, Q_DEV, WIDTH), bf16), ((N_COL, P_DEV, WIDTH), bf16)],
        (ids, exchange(payload, ROW + T), position, q_all, p_all),
        1,
    )
    query_loss = loss[0, :PAIR]
    q_back = exchange(q_pay, ROW)
    p_pay, lifted = lax.optimization_barrier((p_pay, lifted))
    p_back = exchange(p_pay, COL)
    back_gain, payload = call(
        up_kernel,
        "up",
        [((SEQS, WIDTH), f32), ((NT, SEQS + 16, HW_DEV), bf16)],
        (q_back, p_back, pooled, gain, low_a, low_b, out_weight),
    )
    residual_gradient, d_context = call(
        final_kernel,
        "final",
        [((TOKENS, WIDTH), bf16), ((TOKENS, HW_DEV), bf16)],
        (exchange(payload, T), side, wi, inv, pooled, gain, back_gain, hidden_a, hidden_b, lifted),
    )
    return (query_loss, residual_gradient, d_context)


def solution(mesh):
    fine = Mesh(
        mesh.devices.reshape(NZ, NX, NYH, NYL, NC), ("z", "x", "yh", "yl", "core")
    )
    dp = ("z", "x", "yh")
    in_specs = (
        P(dp, T),
        P(dp, T),
        P(None, T),
        P(T),
        P(dp),
        P(dp),
        P(dp),
        P(),
    )
    out_specs = (P(dp + T), P(dp, T), P(dp, T))
    return jax.shard_map(body, mesh=fine, in_specs=in_specs, out_specs=out_specs, check_vma=False)
```

```python
import functools

import jax
import jax.numpy as jnp
from jax import lax
from jax.experimental import pallas as pl
from jax.experimental.pallas import tpu as pltpu
from jax.sharding import Mesh
from jax.sharding import PartitionSpec as P

Q_DEV = 16
P_DEV = 16
SEQ_LEN = 16
SEQS = Q_DEV + P_DEV
TOKENS = SEQS * SEQ_LEN
HALF = TOKENS // 2

EPS = 1e-06
LOGIT_SCALE = 20.0
LOSS_SCALE = 1024.0

NZ, NX, NYH, NYL, NC = 8, 4, 2, 4, 2
NT = NYL * NC
T = ("yl", "core")
ROW = ("x",)
COL = ("z", "yh")
N_ROW = NX
N_COL = NZ * NYH
ROWS = N_ROW * Q_DEV
COLS = N_COL * P_DEV
SHARE = ROWS // NT
PAIR = Q_DEV // NT
HW_DEV = 256
WIDTH = 512
FULL = WIDTH * NT
CAP = 352
CAP_PAD = 384

f32 = jnp.float32
bf16 = jnp.bfloat16
i32 = jnp.int32


def dot(a, b, dims=((1,), (0,)), exact=False):
    return lax.dot_general(
        a,
        b,
        (dims, ((), ())),
        preferred_element_type=f32,
        precision=lax.Precision.HIGHEST if exact else None,
    )


def iota(shape, dim):
    return lax.broadcasted_iota(i32, shape, dim)


def to_col(row, n):
    eye = iota((n, n), 0) == iota((n, n), 1)
    return jnp.sum(jnp.where(eye, row, 0.0), axis=1, keepdims=True)


def to_row(col, n):
    eye = iota((n, n), 0) == iota((n, n), 1)
    return jnp.sum(jnp.where(eye, col, 0.0), axis=0, keepdims=True)


def seg_mask():
    return iota((SEQS, TOKENS), 1) // SEQ_LEN == iota((SEQS, TOKENS), 0)


def split(value):
    high = value.astype(bf16).astype(f32)
    return high, value - high


def row_order():
    shape = (ROWS, ROWS)
    here, there = iota(shape, 0), iota(shape, 1)
    k, x, j = here // SHARE, (here % SHARE) // PAIR, here % PAIR
    return (there == x * Q_DEV + k * PAIR + j).astype(f32).astype(bf16)


def hidden_kernel(last, ids, own, other, weight, residual, *refs):
    if last:
        before, hidden, low, payload = refs
    else:
        hidden, low, payload = refs
    core = ids[0]
    total = residual[HALF * last : HALF * (last + 1), :].astype(f32)
    for y in range(NYL):
        part = slice(y * HW_DEV, (y + 1) * HW_DEV)
        for ref, c in ((own, core), (other, 1 - core)):
            first = pl.multiple_of((y * NC + c) * HW_DEV, HW_DEV)
            total = total + dot(ref[:, part], weight[pl.ds(first, HW_DEV), :])
    hidden[...] = total
    low[...] = total.astype(bf16)
    square = jnp.sum(total * total, axis=1, keepdims=True)
    rows = [to_row(square[b * 128 : (b + 1) * 128], 128) for b in range(HALF // 128)]
    if last:
        rows = [before[0:1], before[1:2]] + rows + [jnp.zeros((4, 128), f32)]
        payload[...] = jnp.broadcast_to(jnp.concatenate(rows, axis=0)[None], (NT, 8, 128))
    else:
        payload[...] = jnp.concatenate(rows + [jnp.zeros((6, 128), f32)], axis=0)


def compact_kernel(q_len, p_len, context, out, dest):
    lengths = jnp.concatenate(
        [to_col(q_len[...].astype(f32), Q_DEV), to_col(p_len[...].astype(f32), P_DEV)], axis=0
    )
    by_lane = to_row(lengths, SEQS)
    before = iota((SEQS, SEQS), 1) < iota((SEQS, SEQS), 0)
    first = jnp.sum(jnp.where(before, by_lane, 0.0), axis=1, keepdims=True)
    slot = (iota((SEQS, TOKENS), 1) % SEQ_LEN).astype(f32)
    row = jnp.where(seg_mask() & (slot < lengths), first + slot + 1.0, 0.0)
    row = jnp.sum(row, axis=0, keepdims=True) - 1.0
    dest[...] = jnp.broadcast_to(row, (8, TOKENS))
    chosen = (iota((CAP, TOKENS), 0).astype(f32) == row).astype(f32).astype(bf16)
    out[...] = dot(chosen, context[...]).astype(bf16)


def few_kernel(ids, own, other, weight, residual, dest, hidden_a, hidden_b, low_a, low_b, payload):
    core = ids[0]
    total = jnp.zeros((CAP, WIDTH), f32)
    for y in range(NYL):
        part = slice(y * HW_DEV, (y + 1) * HW_DEV)
        for ref, c in ((own, core), (other, 1 - core)):
            first = pl.multiple_of((y * NC + c) * HW_DEV, HW_DEV)
            total = total + dot(ref[:, part], weight[pl.ds(first, HW_DEV), :])
    total = jnp.concatenate([total, jnp.zeros((CAP_PAD - CAP, WIDTH), f32)], axis=0)
    high, rest = split(total)
    high, rest = high.astype(bf16), rest.astype(bf16)
    rows = []
    for b in range(TOKENS // 128):
        part = slice(b * 128, (b + 1) * 128)
        inner = slice(b * 128 % HALF, b * 128 % HALF + 128)
        column = to_col(dest[0:1, part], 128)
        chosen = (iota((128, CAP_PAD), 1).astype(f32) == column).astype(f32).astype(bf16)
        block = dot(chosen, high) + dot(chosen, rest) + residual[part, :].astype(f32)
        (hidden_a, hidden_b)[b * 128 // HALF][inner, :] = block
        (low_a, low_b)[b * 128 // HALF][inner, :] = block.astype(bf16)
        rows.append(to_row(jnp.sum(block * block, axis=1, keepdims=True), 128))
    rows = jnp.concatenate(rows + [jnp.zeros((4, 128), f32)], axis=0)
    payload[...] = jnp.broadcast_to(rows[None], (NT, 8, 128))


def pool_kernel(
    squares, q_len, p_len, position, gain, hidden_a, hidden_b, state, lift, q_pay, p_pay
):
    total = jnp.sum(squares[...], axis=0)
    total = jnp.concatenate([total[b : b + 1] for b in range(TOKENS // 128)], axis=1)
    inverse = lax.rsqrt(total / FULL + EPS)
    lengths = jnp.concatenate(
        [to_col(q_len[...].astype(f32), Q_DEV), to_col(p_len[...].astype(f32), P_DEV)], axis=0
    )
    slot = (iota((SEQS, TOKENS), 1) % SEQ_LEN).astype(f32)
    weight = jnp.where(seg_mask() & (slot < lengths), 1.0 / lengths, 0.0) * inverse
    value = dot(weight[:, :HALF], hidden_a[...], exact=True)
    value = value + dot(weight[:, HALF:], hidden_b[...], exact=True)
    value = value * gain[...]
    state[:SEQS, :] = weight
    state[SEQS : 2 * SEQS, :] = value
    state[2 * SEQS :, :] = jnp.concatenate([inverse, gain[...], jnp.zeros((6, WIDTH), f32)], axis=0)
    lift[...] = (value * gain[...]).astype(bf16)
    low = value.astype(bf16)
    where = to_col(position[...].astype(f32), Q_DEV)
    high = jnp.floor(where * (1.0 / 32.0))
    lane = iota((Q_DEV, 128), 1)
    where = jnp.where(lane == 0, high, jnp.where(lane == 1, where - 32.0 * high, 0.0))
    q_pay[:, :, :WIDTH] = jnp.broadcast_to(low[None, :Q_DEV], (N_ROW, Q_DEV, WIDTH))
    q_pay[:, :, WIDTH:] = jnp.broadcast_to(where.astype(bf16)[None], (N_ROW, Q_DEV, 128))
    p_pay[...] = jnp.broadcast_to(low[None, Q_DEV:], (N_COL, P_DEV, WIDTH))


def lift_kernel(low_a, low_b, pooled, weight, out):
    for n in range(NT):
        part = slice(n * HW_DEV, (n + 1) * HW_DEV)
        w = weight[part, :]
        out[:HALF, part] = dot(low_a[...], w, ((1,), (1,))).astype(bf16)
        out[HALF:TOKENS, part] = dot(low_b[...], w, ((1,), (1,))).astype(bf16)
        out[TOKENS:, part] = dot(pooled[...], w, ((1,), (1,))).astype(bf16)


def score_kernel(q_all, p_all, state, lift, low_a, low_b, payload, position):
    order = row_order()
    q_rows = dot(order, q_all[...].reshape(ROWS, WIDTH + 128))
    position[...] = q_rows[:, WIDTH:]
    q_rows = q_rows[:, :WIDTH]
    p_cols = p_all[...].reshape(COLS, WIDTH)
    scores = dot(q_rows.astype(bf16), p_cols, ((1,), (1,)))
    payload[:, :, :COLS] = scores.reshape(NT, SHARE, COLS)
    q_sq = to_row(jnp.sum(q_rows * q_rows, axis=1, keepdims=True), ROWS)
    p_wide = p_cols.astype(f32)
    p_sq = jnp.sum(p_wide * p_wide, axis=1, keepdims=True)
    own = state[SEQS : 2 * SEQS, :]
    own_sq = to_row(jnp.sum(own * own, axis=1, keepdims=True), SEQS)
    cross = [dot(lift[...], low[...], ((1,), (1,))) for low in (low_a, low_b)]
    cross = jnp.sum(jnp.where(seg_mask(), jnp.concatenate(cross, axis=1), 0.0), axis=0, keepdims=True)
    rows = [to_row(p_sq[b * 128 : (b + 1) * 128], 128) for b in range(COLS // 128)]
    rows += [cross[:, b * 128 : (b + 1) * 128] for b in range(TOKENS // 128)]
    rows.append(jnp.concatenate([own_sq, jnp.zeros((1, 128 - SEQS), f32)], axis=1))
    rows.append(jnp.concatenate([q_sq, jnp.zeros((1, 128 - ROWS), f32)], axis=1))
    payload[:, :, COLS:] = jnp.broadcast_to(jnp.concatenate(rows, axis=0)[None], (NT, 8, 128))


def at_positive(position, x):
    where = position[:, 0:1] * 32.0 + position[:, 1:2]
    col = iota((position.shape[0], COLS), 1)
    passage = (col // 32) * 128 + x * 32 + col % 32
    return passage.astype(f32) == where


def softmax_kernel(ids, tile_mask, parts, position, payload, side):
    me, z, x = ids[1], ids[2], ids[3]
    total = jnp.sum(parts[...], axis=0)
    side[...] = total[:, COLS:]
    block = total[:, COLS:]
    scores = total[:, :COLS]
    p_sq = jnp.concatenate([block[0:1], block[1:2]], axis=1)
    own = iota((SHARE, 128), 1) == me * SHARE + iota((SHARE, 128), 0)
    q_sq = jnp.sum(jnp.where(own, block[7:8], 0.0), axis=1, keepdims=True)
    rn = lax.rsqrt(q_sq + EPS) * lax.rsqrt(p_sq + EPS)
    logits = LOGIT_SCALE * scores * rn
    block_of = iota((SHARE, COLS), 1) // 32
    allowed = jnp.zeros((SHARE, COLS), f32)
    for j in range(NZ):
        allowed = jnp.where(block_of == j, tile_mask[z, j].astype(f32), allowed)
    first = pl.multiple_of(me * SHARE, SHARE)
    is_pos = at_positive(position[pl.ds(first, SHARE), :], x)
    expo = jnp.exp(logits)
    others = jnp.where(is_pos, 0.0, expo * allowed)
    sums = [
        jnp.sum(others, axis=1, keepdims=True),
        jnp.sum(jnp.where(is_pos, expo, 0.0), axis=1, keepdims=True),
        jnp.sum(jnp.where(is_pos, logits, 0.0), axis=1, keepdims=True),
    ]
    lane = iota((SHARE, COLS), 1)
    row = jnp.zeros((SHARE, COLS), f32)
    for i, value in enumerate(sums):
        high, rest = split(value)
        middle, low = split(rest)
        for j, piece in enumerate((high, middle, low)):
            row = jnp.where(lane == 3 * i + j, piece, row)
    terms = rn * jnp.where(is_pos, 1.0, others)
    payload[...] = jnp.broadcast_to(
        jnp.concatenate([terms, row], axis=0).astype(bf16)[None], payload.shape
    )


def back_kernel(ids, parts, position, q_all, p_all, loss, q_pay, p_pay):
    me, x = ids[1], ids[3]
    total = jnp.zeros((NT, SHARE, 128), f32)
    for k in range(N_ROW):
        total = total + parts[k * NT : (k + 1) * NT, :, :128].astype(f32)[:, SHARE:, :]
    total = total.reshape(ROWS, 128)
    lane = iota((ROWS, 128), 1)
    others, positive, logit = (
        jnp.sum(jnp.where(lane // 3 == i, total, 0.0), axis=1, keepdims=True) for i in range(3)
    )
    denom = others + positive
    losses = jnp.log(denom) - logit
    row = me * SHARE + x * PAIR + iota((ROWS, 128), 1)
    mine = (iota((ROWS, 128), 0) == row) & (lane < PAIR)
    loss[...] = jnp.broadcast_to(
        jnp.sum(jnp.where(mine, losses, 0.0), axis=0, keepdims=True), loss.shape
    )
    first = pl.multiple_of(x * NT, NT)
    terms = parts[pl.ds(first, NT)].astype(f32)[:, :SHARE, :].reshape(ROWS, COLS)
    factor = LOSS_SCALE / denom
    terms = terms * jnp.where(at_positive(position[...], x), -factor * others, factor)
    terms = dot(row_order(), terms.astype(bf16), ((0,), (0,))).astype(bf16)
    d_q = dot(terms, p_all[...].reshape(COLS, WIDTH))
    q_pay[...] = d_q.astype(bf16).reshape(N_ROW, Q_DEV, WIDTH)
    d_p = dot(terms, q_all[...].reshape(ROWS, WIDTH + 128)[:, :WIDTH], ((0,), (0,)))
    p_pay[...] = d_p.astype(bf16).reshape(N_COL, P_DEV, WIDTH)


def up_kernel(q_parts, p_parts, state, low_a, low_b, weight, back_gain, payload):
    back = jnp.concatenate(
        [jnp.sum(q_parts[...].astype(f32), axis=0), jnp.sum(p_parts[...].astype(f32), axis=0)],
        axis=0,
    )
    inner = to_row(jnp.sum(state[SEQS : 2 * SEQS, :] * back, axis=1, keepdims=True), SEQS)
    scaled = back * state[2 * SEQS + 1 : 2 * SEQS + 2, :]
    back_gain[...] = scaled
    scaled = scaled.astype(bf16)
    cross = [dot(scaled, low[...], ((1,), (1,))) for low in (low_a, low_b)]
    cross = jnp.sum(jnp.where(seg_mask(), jnp.concatenate(cross, axis=1), 0.0), axis=0, keepdims=True)
    inner = jnp.concatenate([inner, jnp.zeros((1, HW_DEV - SEQS), f32)], axis=1)
    rows = jnp.concatenate([cross[:, :HW_DEV], cross[:, HW_DEV:], inner, jnp.zeros((5, HW_DEV), f32)], axis=0)
    high, low = split(rows)
    side = jnp.concatenate([high, low], axis=0).astype(bf16)
    for n in range(NT):
        w = weight[n * HW_DEV : (n + 1) * HW_DEV, :]
        payload[n, :SEQS, :] = dot(scaled, w, ((1,), (1,))).astype(bf16)
        payload[n, SEQS:, :] = side


def final_kernel(parts, side, state, back_gain, hidden_a, hidden_b, lifted, d_res, d_ctx):
    total = jnp.sum(parts[...].astype(f32), axis=0)
    rows = total[SEQS : SEQS + 8] + total[SEQS + 8 :]
    cross_back = jnp.concatenate([rows[0:1], rows[1:2]], axis=1)
    inner = rows[2:3, :SEQS]
    block = side[...]
    cross = jnp.concatenate([block[b : b + 1] for b in range(2, 6)], axis=1)
    ratio = to_col(inner / (block[6:7, :SEQS] + EPS), SEQS)
    lead = LOGIT_SCALE * state[:SEQS, :]
    inverse = state[2 * SEQS : 2 * SEQS + 1, :]
    gain = state[2 * SEQS + 1 : 2 * SEQS + 2, :]
    by_token = jnp.sum(lead * (cross_back - ratio * cross), axis=0, keepdims=True)
    trail = inverse * inverse * by_token / FULL
    d_pooled = back_gain[...] - ratio * (state[SEQS : 2 * SEQS, :] * gain)
    seq_up = total[:SEQS] - ratio * lifted[TOKENS:, :].astype(f32)
    both = jnp.concatenate([d_pooled, seq_up], axis=1)
    for b in range(TOKENS // 128):
        part = slice(b * 128, (b + 1) * 128)
        hidden = (hidden_a, hidden_b)[b * 128 // HALF]
        inner_part = slice(b * 128 % HALF, b * 128 % HALF + 128)
        spread = dot(lead[:, part], both, ((0,), (0,)), exact=True)
        column = to_col(trail[:, part], 128)
        d_res[part, :] = (spread[:, :WIDTH] - column * hidden[inner_part, :]).astype(bf16)
        d_ctx[part, :] = (spread[:, WIDTH:] - column * lifted[part, :].astype(f32)).astype(bf16)


VMEM = pl.BlockSpec()
SMEM = pl.BlockSpec(memory_space=pltpu.SMEM)


def call(kernel, name, outs, args, scalars=0, flops=1 << 20):
    out = [jax.ShapeDtypeStruct(shape, dtype) for shape, dtype in outs]
    size = sum(a.size * a.dtype.itemsize for a in (*args, *out))
    return pl.pallas_call(
        kernel,
        out_shape=out,
        in_specs=[SMEM] * scalars + [VMEM] * (len(args) - scalars),
        out_specs=[VMEM] * len(out),
        compiler_params=pltpu.CompilerParams(vmem_limit_bytes=16 << 20),
        cost_estimate=pl.CostEstimate(flops=flops, bytes_accessed=size, transcendentals=0),
        name=name,
    )(*args)


def exchange(parts, axes):
    return lax.all_to_all(parts, axes, 0, 0)


def hidden_all(ids, out_weight, residual, context):
    parts = []
    for first in (0, HALF):
        own = lax.all_gather(context[first : first + HALF], "yl", axis=1, tiled=True)
        parts.append((own, lax.ppermute(own, "core", [(0, 1), (1, 0)])))
    hidden_outs = [((HALF, WIDTH), f32), ((HALF, WIDTH), bf16)]
    hidden_a, low_a, squares = call(
        functools.partial(hidden_kernel, 0),
        "hidden_a",
        hidden_outs + [((8, 128), f32)],
        (ids, *parts[0], out_weight, residual),
        1,
        flops=2 * HALF * 2048 * WIDTH,
    )
    hidden_b, low_b, squares = call(
        functools.partial(hidden_kernel, 1),
        "hidden_b",
        hidden_outs + [((NT, 8, 128), f32)],
        (ids, *parts[1], out_weight, residual, squares),
        1,
        flops=2 * HALF * 2048 * WIDTH,
    )
    return hidden_a, hidden_b, low_a, low_b, squares


def hidden_few(ids, out_weight, residual, compacted, dest):
    own = lax.all_gather(compacted, "yl", axis=1, tiled=True)
    other = lax.ppermute(own, "core", [(0, 1), (1, 0)])
    return tuple(
        call(
            few_kernel,
            "hidden",
            [((HALF, WIDTH), f32)] * 2 + [((HALF, WIDTH), bf16)] * 2 + [((NT, 8, 128), f32)],
            (ids, own, other, out_weight, residual, dest),
            1,
            flops=2 * CAP * 2048 * WIDTH,
        )
    )


def body(
    context,
    residual,
    out_weight,
    final_norm_weight,
    query_lengths,
    passage_lengths,
    positive_index,
    tile_mask,
):
    me = lax.axis_index(T)
    ids = jnp.stack(
        [lax.axis_index("core"), me, lax.axis_index("z"), lax.axis_index("x")]
    ).astype(i32)
    gain = final_norm_weight.reshape(1, WIDTH)

    compacted, dest = call(
        compact_kernel,
        "compact",
        [((CAP, HW_DEV), bf16), ((8, TOKENS), f32)],
        (query_lengths.reshape(1, Q_DEV), passage_lengths.reshape(1, P_DEV), context),
        flops=2 * CAP * TOKENS * HW_DEV,
    )
    used = jnp.sum(jnp.concatenate([query_lengths, passage_lengths]))
    hidden_a, hidden_b, low_a, low_b, squares = lax.cond(
        used <= CAP,
        functools.partial(hidden_few, ids, out_weight, residual, compacted, dest),
        functools.partial(hidden_all, ids, out_weight, residual, context),
    )
    squares = exchange(squares, T)

    state, lift, q_pay, p_pay = call(
        pool_kernel,
        "pool",
        [
            ((2 * SEQS + 8, WIDTH), f32),
            ((SEQS, WIDTH), bf16),
            ((N_ROW, Q_DEV, WIDTH + 128), bf16),
            ((N_COL, P_DEV, WIDTH), bf16),
        ],
        (
            squares,
            query_lengths.reshape(1, Q_DEV),
            passage_lengths.reshape(1, P_DEV),
            positive_index.reshape(1, Q_DEV),
            gain,
            hidden_a,
            hidden_b,
        ),
    )
    q_all = exchange(q_pay, ROW)
    (lifted,) = call(
        lift_kernel,
        "lift",
        [((TOKENS + SEQS, NT * HW_DEV), bf16)],
        (low_a, low_b, lift, out_weight),
        flops=2 * TOKENS * 2048 * WIDTH,
    )
    p_all = exchange(p_pay, COL)

    payload, position = call(
        score_kernel,
        "score",
        [((NT, SHARE, COLS + 128), f32), ((ROWS, 128), f32)],
        (q_all, p_all, state, lift, low_a, low_b),
    )
    payload, lifted = lax.optimization_barrier((payload, lifted))
    lifted = lax.psum_scatter(lifted, T, scatter_dimension=1, tiled=True)
    payload, side = call(
        softmax_kernel,
        "softmax",
        [((N_ROW * NT, 2 * SHARE, COLS), bf16), ((SHARE, 128), f32)],
        (ids, tile_mask, exchange(payload, T), position),
        2,
    )
    loss, q_pay, p_pay = call(
        back_kernel,
        "back",
        [((8, 128), f32), ((N_ROW, Q_DEV, WIDTH), bf16), ((N_COL, P_DEV, WIDTH), bf16)],
        (ids, exchange(payload, ROW + T), position, q_all, p_all),
        1,
    )
    query_loss = loss[0, :PAIR]
    q_back = exchange(q_pay, ROW)
    p_back = exchange(p_pay, COL)
    back_gain, payload = call(
        up_kernel,
        "up",
        [((SEQS, WIDTH), f32), ((NT, SEQS + 16, HW_DEV), bf16)],
        (q_back, p_back, state, low_a, low_b, out_weight),
    )
    payload, lifted = lax.optimization_barrier((payload, lifted))
    residual_gradient, d_context = call(
        final_kernel,
        "final",
        [((TOKENS, WIDTH), bf16), ((TOKENS, HW_DEV), bf16)],
        (exchange(payload, T), side, state, back_gain, hidden_a, hidden_b, lifted),
    )
    return (query_loss, residual_gradient, d_context)


def solution(mesh):
    fine = Mesh(
        mesh.devices.reshape(NZ, NX, NYH, NYL, NC), ("z", "x", "yh", "yl", "core")
    )
    dp = ("z", "x", "yh")
    in_specs = (
        P(dp, T),
        P(dp, T),
        P(None, T),
        P(T),
        P(dp),
        P(dp),
        P(dp),
        P(),
    )
    out_specs = (P(dp + T), P(dp, T), P(dp, T))
    return jax.shard_map(body, mesh=fine, in_specs=in_specs, out_specs=out_specs, check_vma=False)
```

```python
import functools

import jax
import jax.numpy as jnp
from jax import lax
from jax.experimental import pallas as pl
from jax.experimental.pallas import tpu as pltpu
from jax.sharding import Mesh
from jax.sharding import PartitionSpec as P

Q_DEV = 16
P_DEV = 16
SEQ_LEN = 16
SEQS = Q_DEV + P_DEV
TOKENS = SEQS * SEQ_LEN
HALF = TOKENS // 2

EPS = 1e-06
LOGIT_SCALE = 20.0
LOSS_SCALE = 1024.0

NZ, NX, NYH, NYL, NC = 8, 4, 2, 4, 2
NT = NYL * NC
T = ("yl", "core")
ROW = ("x",)
COL = ("z", "yh")
N_ROW = NX
N_COL = NZ * NYH
ROWS = N_ROW * Q_DEV
COLS = N_COL * P_DEV
SHARE = ROWS // NT
PAIR = Q_DEV // NT
HW_DEV = 256
WIDTH = 512
FULL = WIDTH * NT
CAP = 352
CAP_PAD = 384

f32 = jnp.float32
bf16 = jnp.bfloat16
i32 = jnp.int32


def dot(a, b, dims=((1,), (0,)), exact=False):
    return lax.dot_general(
        a,
        b,
        (dims, ((), ())),
        preferred_element_type=f32,
        precision=lax.Precision.HIGHEST if exact else None,
    )


def iota(shape, dim):
    return lax.broadcasted_iota(i32, shape, dim)


def to_col(row, n):
    eye = iota((n, n), 0) == iota((n, n), 1)
    return jnp.sum(jnp.where(eye, row, 0.0), axis=1, keepdims=True)


def to_row(col, n):
    eye = iota((n, n), 0) == iota((n, n), 1)
    return jnp.sum(jnp.where(eye, col, 0.0), axis=0, keepdims=True)


def seg_mask():
    return iota((SEQS, TOKENS), 1) // SEQ_LEN == iota((SEQS, TOKENS), 0)


def split(value):
    high = value.astype(bf16).astype(f32)
    return high, value - high


def row_order():
    shape = (ROWS, ROWS)
    here, there = iota(shape, 0), iota(shape, 1)
    k, x, j = here // SHARE, (here % SHARE) // PAIR, here % PAIR
    return (there == x * Q_DEV + k * PAIR + j).astype(f32).astype(bf16)


def hidden_kernel(last, ids, own, other, weight, residual, *refs):
    if last:
        before, hidden, low, payload = refs
    else:
        hidden, low, payload = refs
    core = ids[0]
    total = residual[HALF * last : HALF * (last + 1), :].astype(f32)
    for y in range(NYL):
        part = slice(y * HW_DEV, (y + 1) * HW_DEV)
        for ref, c in ((own, core), (other, 1 - core)):
            first = pl.multiple_of((y * NC + c) * HW_DEV, HW_DEV)
            total = total + dot(ref[:, part], weight[pl.ds(first, HW_DEV), :])
    hidden[...] = total
    low[...] = total.astype(bf16)
    square = jnp.sum(total * total, axis=1, keepdims=True)
    rows = [to_row(square[b * 128 : (b + 1) * 128], 128) for b in range(HALF // 128)]
    if last:
        rows = [before[0:1], before[1:2]] + rows + [jnp.zeros((4, 128), f32)]
        payload[...] = jnp.broadcast_to(jnp.concatenate(rows, axis=0)[None], (NT, 8, 128))
    else:
        payload[...] = jnp.concatenate(rows + [jnp.zeros((6, 128), f32)], axis=0)


def compact_kernel(q_len, p_len, context, out, dest, fits):
    lengths = jnp.concatenate(
        [to_col(q_len[...].astype(f32), Q_DEV), to_col(p_len[...].astype(f32), P_DEV)], axis=0
    )
    by_lane = to_row(lengths, SEQS)
    fits[0, 0] = (jnp.sum(by_lane) <= CAP).astype(i32)
    before = iota((SEQS, SEQS), 1) < iota((SEQS, SEQS), 0)
    first = jnp.sum(jnp.where(before, by_lane, 0.0), axis=1, keepdims=True)
    slot = (iota((SEQS, TOKENS), 1) % SEQ_LEN).astype(f32)
    row = jnp.where(seg_mask() & (slot < lengths), first + slot + 1.0, 0.0)
    row = jnp.sum(row, axis=0, keepdims=True) - 1.0
    dest[...] = jnp.broadcast_to(row, (8, TOKENS))
    chosen = (iota((CAP, TOKENS), 0).astype(f32) == row).astype(f32).astype(bf16)
    out[...] = dot(chosen, context[...]).astype(bf16)


def few_kernel(ids, own, other, weight, residual, dest, hidden, low, payload):
    core = ids[0]
    total = jnp.zeros((CAP, WIDTH), f32)
    for y in range(NYL):
        part = slice(y * HW_DEV, (y + 1) * HW_DEV)
        for ref, c in ((own, core), (other, 1 - core)):
            first = pl.multiple_of((y * NC + c) * HW_DEV, HW_DEV)
            total = total + dot(ref[:, part], weight[pl.ds(first, HW_DEV), :])
    total = jnp.concatenate([total, jnp.zeros((CAP_PAD - CAP, WIDTH), f32)], axis=0)
    high, rest = split(total)
    high, rest = high.astype(bf16), rest.astype(bf16)
    rows = []
    for b in range(TOKENS // 128):
        part = slice(b * 128, (b + 1) * 128)
        column = to_col(dest[0:1, part], 128)
        chosen = (iota((128, CAP_PAD), 1).astype(f32) == column).astype(f32).astype(bf16)
        block = dot(chosen, high) + dot(chosen, rest) + residual[part, :].astype(f32)
        hidden[part, :] = block
        low[part, :] = block.astype(bf16)
        rows.append(to_row(jnp.sum(block * block, axis=1, keepdims=True), 128))
    rows = jnp.concatenate(rows + [jnp.zeros((4, 128), f32)], axis=0)
    payload[...] = jnp.broadcast_to(rows[None], (NT, 8, 128))


def pool_kernel(
    squares, q_len, p_len, position, gain, hidden, state, lift, q_pay, p_pay
):
    total = jnp.sum(squares[...], axis=0)
    total = jnp.concatenate([total[b : b + 1] for b in range(TOKENS // 128)], axis=1)
    inverse = lax.rsqrt(total / FULL + EPS)
    lengths = jnp.concatenate(
        [to_col(q_len[...].astype(f32), Q_DEV), to_col(p_len[...].astype(f32), P_DEV)], axis=0
    )
    slot = (iota((SEQS, TOKENS), 1) % SEQ_LEN).astype(f32)
    weight = jnp.where(seg_mask() & (slot < lengths), 1.0 / lengths, 0.0) * inverse
    value = dot(weight, hidden[...], exact=True) * gain[...]
    state[:SEQS, :] = weight
    state[SEQS : 2 * SEQS, :] = value
    state[2 * SEQS :, :] = jnp.concatenate([inverse, gain[...], jnp.zeros((6, WIDTH), f32)], axis=0)
    lift[...] = (value * gain[...]).astype(bf16)
    low = value.astype(bf16)
    where = to_col(position[...].astype(f32), Q_DEV)
    high = jnp.floor(where * (1.0 / 32.0))
    lane = iota((Q_DEV, 128), 1)
    where = jnp.where(lane == 0, high, jnp.where(lane == 1, where - 32.0 * high, 0.0))
    q_pay[:, :, :WIDTH] = jnp.broadcast_to(low[None, :Q_DEV], (N_ROW, Q_DEV, WIDTH))
    q_pay[:, :, WIDTH:] = jnp.broadcast_to(where.astype(bf16)[None], (N_ROW, Q_DEV, 128))
    p_pay[...] = jnp.broadcast_to(low[None, Q_DEV:], (N_COL, P_DEV, WIDTH))


def lift_kernel(low, pooled, weight, out):
    out[:TOKENS, :] = dot(low[...], weight[...], ((1,), (1,))).astype(bf16)
    out[TOKENS:, :] = dot(pooled[...], weight[...], ((1,), (1,))).astype(bf16)


def score_kernel(q_all, p_all, state, lift, low, payload, position):
    order = row_order()
    q_rows = dot(order, q_all[...].reshape(ROWS, WIDTH + 128))
    position[...] = q_rows[:, WIDTH:]
    q_rows = q_rows[:, :WIDTH]
    p_cols = p_all[...].reshape(COLS, WIDTH)
    scores = dot(q_rows.astype(bf16), p_cols, ((1,), (1,)))
    payload[:, :, :COLS] = scores.reshape(NT, SHARE, COLS)
    q_sq = to_row(jnp.sum(q_rows * q_rows, axis=1, keepdims=True), ROWS)
    p_wide = p_cols.astype(f32)
    p_sq = jnp.sum(p_wide * p_wide, axis=1, keepdims=True)
    own = state[SEQS : 2 * SEQS, :]
    own_sq = to_row(jnp.sum(own * own, axis=1, keepdims=True), SEQS)
    cross = dot(lift[...], low[...], ((1,), (1,)))
    cross = jnp.sum(jnp.where(seg_mask(), cross, 0.0), axis=0, keepdims=True)
    rows = [to_row(p_sq[b * 128 : (b + 1) * 128], 128) for b in range(COLS // 128)]
    rows += [cross[:, b * 128 : (b + 1) * 128] for b in range(TOKENS // 128)]
    rows.append(jnp.concatenate([own_sq, jnp.zeros((1, 128 - SEQS), f32)], axis=1))
    rows.append(jnp.concatenate([q_sq, jnp.zeros((1, 128 - ROWS), f32)], axis=1))
    payload[:, :, COLS:] = jnp.broadcast_to(jnp.concatenate(rows, axis=0)[None], (NT, 8, 128))


def at_positive(position, x):
    where = position[:, 0:1] * 32.0 + position[:, 1:2]
    col = iota((position.shape[0], COLS), 1)
    passage = (col // 32) * 128 + x * 32 + col % 32
    return passage.astype(f32) == where


def softmax_kernel(ids, tile_mask, parts, position, payload, side):
    me, z, x = ids[1], ids[2], ids[3]
    total = jnp.sum(parts[...], axis=0)
    side[...] = total[:, COLS:]
    block = total[:, COLS:]
    scores = total[:, :COLS]
    p_sq = jnp.concatenate([block[0:1], block[1:2]], axis=1)
    own = iota((SHARE, 128), 1) == me * SHARE + iota((SHARE, 128), 0)
    q_sq = jnp.sum(jnp.where(own, block[7:8], 0.0), axis=1, keepdims=True)
    rn = lax.rsqrt(q_sq + EPS) * lax.rsqrt(p_sq + EPS)
    logits = LOGIT_SCALE * scores * rn
    block_of = iota((SHARE, COLS), 1) // 32
    allowed = jnp.zeros((SHARE, COLS), f32)
    for j in range(NZ):
        allowed = jnp.where(block_of == j, tile_mask[z, j].astype(f32), allowed)
    first = pl.multiple_of(me * SHARE, SHARE)
    is_pos = at_positive(position[pl.ds(first, SHARE), :], x)
    expo = jnp.exp(logits)
    others = jnp.where(is_pos, 0.0, expo * allowed)
    sums = [
        jnp.sum(others, axis=1, keepdims=True),
        jnp.sum(jnp.where(is_pos, expo, 0.0), axis=1, keepdims=True),
        jnp.sum(jnp.where(is_pos, logits, 0.0), axis=1, keepdims=True),
    ]
    lane = iota((SHARE, COLS), 1)
    row = jnp.zeros((SHARE, COLS), f32)
    for i, value in enumerate(sums):
        high, rest = split(value)
        middle, low = split(rest)
        for j, piece in enumerate((high, middle, low)):
            row = jnp.where(lane == 3 * i + j, piece, row)
    terms = rn * jnp.where(is_pos, 1.0, others)
    payload[...] = jnp.broadcast_to(
        jnp.concatenate([terms, row], axis=0).astype(bf16)[None], payload.shape
    )


def query_kernel(ids, parts, q_all, p_all, payload, terms_out):
    x = ids[3]
    value = parts[...].astype(f32)
    order = row_order()
    terms = value[:, :SHARE, :].reshape(ROWS, COLS).astype(bf16)
    terms = dot(order, terms, ((0,), (0,)))
    sums = value[:, SHARE:, :128].reshape(ROWS, 128).astype(bf16)
    sums = dot(order, sums, ((0,), (0,)))
    low = terms.astype(bf16)
    terms_out[...] = low
    at_pos = at_positive(q_all[...].reshape(ROWS, WIDTH + 128)[:, WIDTH:].astype(f32), x)
    p_cols = p_all[...].reshape(COLS, WIDTH)
    others = dot(jnp.where(at_pos, 0.0, terms).astype(bf16), p_cols)
    positive = dot(jnp.where(at_pos, terms, 0.0).astype(bf16), p_cols)
    payload[:, :Q_DEV, :] = others.astype(bf16).reshape(N_ROW, Q_DEV, WIDTH)
    payload[:, Q_DEV : 2 * Q_DEV, :] = positive.astype(bf16).reshape(N_ROW, Q_DEV, WIDTH)
    sums = jnp.concatenate([sums[k * Q_DEV : (k + 1) * Q_DEV] for k in range(N_ROW)], axis=1)
    payload[:, 2 * Q_DEV :, :] = jnp.broadcast_to(sums.astype(bf16)[None], (N_ROW, Q_DEV, WIDTH))


def passage_kernel(ids, parts, terms, q_all, loss, back_q, payload):
    me, x = ids[1], ids[3]
    total = jnp.sum(parts[...].astype(f32), axis=0)
    sums = total[2 * Q_DEV :]
    sums = jnp.concatenate([sums[:, k * 128 : (k + 1) * 128] for k in range(N_ROW)], axis=0)
    lane = iota((ROWS, 128), 1)
    others, positive, logit = (
        jnp.sum(jnp.where(lane // 3 == i, sums, 0.0), axis=1, keepdims=True) for i in range(3)
    )
    denom = others + positive
    losses = jnp.log(denom) - logit
    mine = (iota((ROWS, 128), 0) == x * Q_DEV + me * PAIR + lane) & (lane < PAIR)
    loss[...] = jnp.broadcast_to(
        jnp.sum(jnp.where(mine, losses, 0.0), axis=0, keepdims=True), loss.shape
    )
    factor = LOSS_SCALE / denom
    own_factor = jnp.zeros((Q_DEV, 1), f32)
    own_others = jnp.zeros((Q_DEV, 1), f32)
    for k in range(N_ROW):
        rows = slice(k * Q_DEV, (k + 1) * Q_DEV)
        own_factor = jnp.where(x == k, factor[rows], own_factor)
        own_others = jnp.where(x == k, others[rows], own_others)
    back_q[...] = own_factor * (total[:Q_DEV] - own_others * total[Q_DEV : 2 * Q_DEV])
    q_wide = q_all[...].reshape(ROWS, WIDTH + 128)
    at_pos = at_positive(q_wide[:, WIDTH:].astype(f32), x)
    value = terms[...].astype(f32) * jnp.where(at_pos, -factor * others, factor)
    d_p = dot(value.astype(bf16), q_wide[:, :WIDTH], ((0,), (0,)))
    payload[...] = d_p.astype(bf16).reshape(N_COL, P_DEV, WIDTH)


def up_kernel(back_q, p_parts, state, low, weight, back_gain, payload):
    back = jnp.concatenate([back_q[...], jnp.sum(p_parts[...].astype(f32), axis=0)], axis=0)
    inner = to_row(jnp.sum(state[SEQS : 2 * SEQS, :] * back, axis=1, keepdims=True), SEQS)
    scaled = back * state[2 * SEQS + 1 : 2 * SEQS + 2, :]
    back_gain[...] = scaled
    scaled = scaled.astype(bf16)
    cross = dot(scaled, low[...], ((1,), (1,)))
    cross = jnp.sum(jnp.where(seg_mask(), cross, 0.0), axis=0, keepdims=True)
    inner = jnp.concatenate([inner, jnp.zeros((1, HW_DEV - SEQS), f32)], axis=1)
    rows = [cross[:, :HW_DEV], cross[:, HW_DEV:], inner, jnp.zeros((5, HW_DEV), f32)]
    side = jnp.concatenate(split(jnp.concatenate(rows, axis=0)), axis=0).astype(bf16)
    for n in range(NT):
        w = weight[n * HW_DEV : (n + 1) * HW_DEV, :]
        payload[n, :SEQS, :] = dot(scaled, w, ((1,), (1,))).astype(bf16)
        payload[n, SEQS:, :] = side


def final_kernel(parts, side, state, back_gain, hidden, lifted, d_res, d_ctx):
    total = jnp.sum(parts[...].astype(f32), axis=0)
    rows = total[SEQS : SEQS + 8] + total[SEQS + 8 :]
    cross_back = jnp.concatenate([rows[0:1], rows[1:2]], axis=1)
    inner = rows[2:3, :SEQS]
    block = side[...]
    cross = jnp.concatenate([block[b : b + 1] for b in range(2, 6)], axis=1)
    ratio = to_col(inner / (block[6:7, :SEQS] + EPS), SEQS)
    lead = LOGIT_SCALE * state[:SEQS, :]
    inverse = state[2 * SEQS : 2 * SEQS + 1, :]
    gain = state[2 * SEQS + 1 : 2 * SEQS + 2, :]
    by_token = jnp.sum(lead * (cross_back - ratio * cross), axis=0, keepdims=True)
    trail = inverse * inverse * by_token / FULL
    d_pooled = back_gain[...] - ratio * (state[SEQS : 2 * SEQS, :] * gain)
    seq_up = total[:SEQS] - ratio * lifted[TOKENS:, :].astype(f32)
    both = jnp.concatenate([d_pooled, seq_up], axis=1)
    for b in range(TOKENS // 128):
        part = slice(b * 128, (b + 1) * 128)
        spread = dot(lead[:, part], both, ((0,), (0,)), exact=True)
        column = to_col(trail[:, part], 128)
        d_res[part, :] = (spread[:, :WIDTH] - column * hidden[part, :]).astype(bf16)
        d_ctx[part, :] = (spread[:, WIDTH:] - column * lifted[part, :].astype(f32)).astype(bf16)


VMEM = pl.BlockSpec()
PINNED = pl.BlockSpec(memory_space=pltpu.VMEM)
SMEM = pl.BlockSpec(memory_space=pltpu.SMEM)


def whole(*shape):
    return pl.BlockSpec(shape, lambda i: (0,) * len(shape))


def call(kernel, name, outs, args, scalars=0, flops=1 << 20, flags=0, pinned=(), **grid):
    out = [jax.ShapeDtypeStruct(shape, dtype) for shape, dtype in outs]
    if not grid:
        grid = dict(
            in_specs=[SMEM] * scalars
            + [PINNED if i in pinned else VMEM for i in range(scalars, len(args))],
            out_specs=[VMEM] * (len(out) - flags) + [SMEM] * flags,
        )
    size = sum(a.size * a.dtype.itemsize for a in (*args, *out))
    return pl.pallas_call(
        kernel,
        out_shape=out,
        **grid,
        compiler_params=pltpu.CompilerParams(vmem_limit_bytes=16 << 20),
        cost_estimate=pl.CostEstimate(flops=flops, bytes_accessed=size, transcendentals=0),
        name=name,
    )(*args)


def exchange(parts, axes):
    return lax.all_to_all(parts, axes, 0, 0)


def hidden_all(ids, out_weight, residual, context):
    parts = []
    for first in (0, HALF):
        own = lax.all_gather(context[first : first + HALF], "yl", axis=1, tiled=True)
        parts.append((own, lax.ppermute(own, "core", [(0, 1), (1, 0)])))
    hidden_outs = [((HALF, WIDTH), f32), ((HALF, WIDTH), bf16)]
    hidden_a, low_a, squares = call(
        functools.partial(hidden_kernel, 0),
        "hidden_a",
        hidden_outs + [((8, 128), f32)],
        (ids, *parts[0], out_weight, residual),
        1,
        flops=2 * HALF * 2048 * WIDTH,
    )
    hidden_b, low_b, squares = call(
        functools.partial(hidden_kernel, 1),
        "hidden_b",
        hidden_outs + [((NT, 8, 128), f32)],
        (ids, *parts[1], out_weight, residual, squares),
        1,
        flops=2 * HALF * 2048 * WIDTH,
    )
    hidden = jnp.concatenate([hidden_a, hidden_b], axis=0)
    low = jnp.concatenate([low_a, low_b], axis=0)
    return hidden, low, squares


def hidden_few(ids, out_weight, residual, compacted, dest):
    own = lax.all_gather(compacted, "yl", axis=1, tiled=True)
    other = lax.ppermute(own, "core", [(0, 1), (1, 0)])
    return tuple(
        call(
            few_kernel,
            "hidden",
            [((TOKENS, WIDTH), f32), ((TOKENS, WIDTH), bf16), ((NT, 8, 128), f32)],
            (ids, own, other, out_weight, residual, dest),
            1,
            flops=2 * CAP * 2048 * WIDTH,
        )
    )


def body(
    context,
    residual,
    out_weight,
    final_norm_weight,
    query_lengths,
    passage_lengths,
    positive_index,
    tile_mask,
):
    me = lax.axis_index(T)
    ids = jnp.stack(
        [lax.axis_index("core"), me, lax.axis_index("z"), lax.axis_index("x")]
    ).astype(i32)
    gain = final_norm_weight.reshape(1, WIDTH)

    compacted, dest, fits = call(
        compact_kernel,
        "compact",
        [((CAP, HW_DEV), bf16), ((8, TOKENS), f32), ((1, 1), i32)],
        (query_lengths.reshape(1, Q_DEV), passage_lengths.reshape(1, P_DEV), context),
        flops=2 * CAP * TOKENS * HW_DEV,
        flags=1,
    )
    hidden, low, squares = lax.cond(
        fits[0, 0] == 1,
        functools.partial(hidden_few, ids, out_weight, residual, compacted, dest),
        functools.partial(hidden_all, ids, out_weight, residual, context),
    )
    squares = exchange(squares, T)

    state, lift, q_pay, p_pay = call(
        pool_kernel,
        "pool",
        [
            ((2 * SEQS + 8, WIDTH), f32),
            ((SEQS, WIDTH), bf16),
            ((N_ROW, Q_DEV, WIDTH + 128), bf16),
            ((N_COL, P_DEV, WIDTH), bf16),
        ],
        (
            squares,
            query_lengths.reshape(1, Q_DEV),
            passage_lengths.reshape(1, P_DEV),
            positive_index.reshape(1, Q_DEV),
            gain,
            hidden,
        ),
    )
    q_all = exchange(q_pay, ROW)
    (lifted,) = call(
        lift_kernel,
        "lift",
        [((TOKENS + SEQS, NT * HW_DEV), bf16)],
        (low, lift, out_weight),
        flops=2 * TOKENS * 2048 * WIDTH,
        grid=(NT // 2,),
        in_specs=[
            whole(TOKENS, WIDTH),
            whole(SEQS, WIDTH),
            pl.BlockSpec((2 * HW_DEV, WIDTH), lambda i: (i, 0)),
        ],
        out_specs=[pl.BlockSpec((TOKENS + SEQS, 2 * HW_DEV), lambda i: (0, i))],
    )
    p_all = exchange(p_pay, COL)

    payload, position = call(
        score_kernel,
        "score",
        [((NT, SHARE, COLS + 128), f32), ((ROWS, 128), f32)],
        (q_all, p_all, state, lift, low),
    )
    payload, lifted = lax.optimization_barrier((payload, lifted))
    lifted = lax.psum_scatter(lifted, T, scatter_dimension=1, tiled=True)
    payload, side = call(
        softmax_kernel,
        "softmax",
        [((NT, 2 * SHARE, COLS), bf16), ((SHARE, 128), f32)],
        (ids, tile_mask, exchange(payload, T), position),
        2,
    )
    payload, terms = call(
        query_kernel,
        "query",
        [((N_ROW, 3 * Q_DEV, WIDTH), bf16), ((ROWS, COLS), bf16)],
        (ids, exchange(payload, T), q_all, p_all),
        1,
    )
    loss, back_q, payload = call(
        passage_kernel,
        "passage",
        [((8, 128), f32), ((Q_DEV, WIDTH), f32), ((N_COL, P_DEV, WIDTH), bf16)],
        (ids, exchange(payload, ROW), terms, q_all),
        1,
    )
    query_loss = loss[0, :PAIR]
    back_gain, payload = call(
        up_kernel,
        "up",
        [((SEQS, WIDTH), f32), ((NT, SEQS + 16, HW_DEV), bf16)],
        (back_q, exchange(payload, COL), state, low, out_weight),
    )
    payload, lifted = lax.optimization_barrier((payload, lifted))
    residual_gradient, d_context = call(
        final_kernel,
        "final",
        [((TOKENS, WIDTH), bf16), ((TOKENS, HW_DEV), bf16)],
        (exchange(payload, T), side, state, back_gain, hidden, lifted),
    )
    return (query_loss, residual_gradient, d_context)


def solution(mesh):
    fine = Mesh(
        mesh.devices.reshape(NZ, NX, NYH, NYL, NC), ("z", "x", "yh", "yl", "core")
    )
    dp = ("z", "x", "yh")
    in_specs = (
        P(dp, T),
        P(dp, T),
        P(None, T),
        P(T),
        P(dp),
        P(dp),
        P(dp),
        P(),
    )
    out_specs = (P(dp + T), P(dp, T), P(dp, T))
    return jax.shard_map(body, mesh=fine, in_specs=in_specs, out_specs=out_specs, check_vma=False)
```

```python
import functools

import jax
import jax.numpy as jnp
from jax import lax
from jax.experimental import pallas as pl
from jax.experimental.pallas import tpu as pltpu
from jax.sharding import Mesh
from jax.sharding import PartitionSpec as P

Q_DEV = 16
P_DEV = 16
SEQ_LEN = 16
SEQS = Q_DEV + P_DEV
TOKENS = SEQS * SEQ_LEN
HALF = TOKENS // 2

EPS = 1e-06
LOGIT_SCALE = 20.0
LOSS_SCALE = 1024.0

NZ, NX, NYH, NYL, NC = 8, 4, 2, 4, 2
NT = NYL * NC
T = ("yl", "core")
ROW = ("x",)
COL = ("z", "yh")
N_ROW = NX
N_COL = NZ * NYH
ROWS = N_ROW * Q_DEV
COLS = N_COL * P_DEV
SHARE = ROWS // NT
PAIR = Q_DEV // NT
HW_DEV = 256
WIDTH = 512
FULL = WIDTH * NT
CAP = 352
CAP_PAD = 384

f32 = jnp.float32
bf16 = jnp.bfloat16
i32 = jnp.int32


def dot(a, b, dims=((1,), (0,)), exact=False):
    return lax.dot_general(
        a,
        b,
        (dims, ((), ())),
        preferred_element_type=f32,
        precision=lax.Precision.HIGHEST if exact else None,
    )


def iota(shape, dim):
    return lax.broadcasted_iota(i32, shape, dim)


def to_col(row, n):
    eye = iota((n, n), 0) == iota((n, n), 1)
    return jnp.sum(jnp.where(eye, row, 0.0), axis=1, keepdims=True)


def to_row(col, n):
    eye = iota((n, n), 0) == iota((n, n), 1)
    return jnp.sum(jnp.where(eye, col, 0.0), axis=0, keepdims=True)


def seg_mask():
    return iota((SEQS, TOKENS), 1) // SEQ_LEN == iota((SEQS, TOKENS), 0)


def split(value):
    high = value.astype(bf16).astype(f32)
    return high, value - high


def row_order():
    shape = (ROWS, ROWS)
    here, there = iota(shape, 0), iota(shape, 1)
    k, x, j = here // SHARE, (here % SHARE) // PAIR, here % PAIR
    return (there == x * Q_DEV + k * PAIR + j).astype(f32).astype(bf16)


def hidden_kernel(last, ids, own, other, weight, residual, *refs):
    if last:
        before, hidden, low, payload = refs
    else:
        hidden, low, payload = refs
    core = ids[0]
    total = residual[HALF * last : HALF * (last + 1), :].astype(f32)
    for y in range(NYL):
        part = slice(y * HW_DEV, (y + 1) * HW_DEV)
        for ref, c in ((own, core), (other, 1 - core)):
            first = pl.multiple_of((y * NC + c) * HW_DEV, HW_DEV)
            total = total + dot(ref[:, part], weight[pl.ds(first, HW_DEV), :])
    hidden[...] = total
    low[...] = total.astype(bf16)
    square = jnp.sum(total * total, axis=1, keepdims=True)
    rows = [to_row(square[b * 128 : (b + 1) * 128], 128) for b in range(HALF // 128)]
    if last:
        rows = [before[0:1], before[1:2]] + rows + [jnp.zeros((4, 128), f32)]
        payload[...] = jnp.broadcast_to(jnp.concatenate(rows, axis=0)[None], (NT, 8, 128))
    else:
        payload[...] = jnp.concatenate(rows + [jnp.zeros((6, 128), f32)], axis=0)


def compact_kernel(q_len, p_len, context, out, dest, fits, q_here, p_here, context_here, sems):
    copies = [
        pltpu.make_async_copy(source, target, sems.at[i])
        for i, (source, target) in enumerate(
            ((q_len, q_here), (p_len, p_here), (context, context_here))
        )
    ]
    for copy in copies:
        copy.start()
    copies[0].wait()
    copies[1].wait()
    lengths = jnp.concatenate(
        [to_col(q_here[...].astype(f32), Q_DEV), to_col(p_here[...].astype(f32), P_DEV)], axis=0
    )
    by_lane = to_row(lengths, SEQS)
    fits[0, 0] = (jnp.sum(by_lane) <= CAP).astype(i32)
    before = iota((SEQS, SEQS), 1) < iota((SEQS, SEQS), 0)
    first = jnp.sum(jnp.where(before, by_lane, 0.0), axis=1, keepdims=True)
    slot = (iota((SEQS, TOKENS), 1) % SEQ_LEN).astype(f32)
    row = jnp.where(seg_mask() & (slot < lengths), first + slot + 1.0, 0.0)
    row = jnp.sum(row, axis=0, keepdims=True) - 1.0
    dest[...] = jnp.broadcast_to(row, (8, TOKENS))
    chosen = (iota((CAP, TOKENS), 0).astype(f32) == row).astype(f32).astype(bf16)
    copies[2].wait()
    out[...] = dot(chosen, context_here[...]).astype(bf16)


def few_kernel(ids, own, other, weight, residual, dest, hidden, low, payload):
    core = ids[0]
    total = jnp.zeros((CAP, WIDTH), f32)
    for y in range(NYL):
        part = slice(y * HW_DEV, (y + 1) * HW_DEV)
        for ref, c in ((own, core), (other, 1 - core)):
            first = pl.multiple_of((y * NC + c) * HW_DEV, HW_DEV)
            total = total + dot(ref[:, part], weight[pl.ds(first, HW_DEV), :])
    total = jnp.concatenate([total, jnp.zeros((CAP_PAD - CAP, WIDTH), f32)], axis=0)
    high, rest = split(total)
    high, rest = high.astype(bf16), rest.astype(bf16)
    rows = []
    for b in range(TOKENS // 128):
        part = slice(b * 128, (b + 1) * 128)
        column = to_col(dest[0:1, part], 128)
        chosen = (iota((128, CAP_PAD), 1).astype(f32) == column).astype(f32).astype(bf16)
        block = dot(chosen, high) + dot(chosen, rest) + residual[part, :].astype(f32)
        hidden[part, :] = block
        low[part, :] = block.astype(bf16)
        rows.append(to_row(jnp.sum(block * block, axis=1, keepdims=True), 128))
    rows = jnp.concatenate(rows + [jnp.zeros((4, 128), f32)], axis=0)
    payload[...] = jnp.broadcast_to(rows[None], (NT, 8, 128))


def pool_kernel(
    squares, q_len, p_len, position, gain, hidden, state, lift, q_pay, p_pay
):
    total = jnp.sum(squares[...], axis=0)
    total = jnp.concatenate([total[b : b + 1] for b in range(TOKENS // 128)], axis=1)
    inverse = lax.rsqrt(total / FULL + EPS)
    lengths = jnp.concatenate(
        [to_col(q_len[...].astype(f32), Q_DEV), to_col(p_len[...].astype(f32), P_DEV)], axis=0
    )
    slot = (iota((SEQS, TOKENS), 1) % SEQ_LEN).astype(f32)
    weight = jnp.where(seg_mask() & (slot < lengths), 1.0 / lengths, 0.0) * inverse
    high, rest = (piece.astype(bf16) for piece in split(weight))
    hidden_high, hidden_rest = (piece.astype(bf16) for piece in split(hidden[...]))
    both = dot(jnp.concatenate([high, rest], axis=0), hidden_high)
    value = (both[:SEQS] + both[SEQS:] + dot(high, hidden_rest)) * gain[...]
    state[:SEQS, :] = weight
    state[SEQS : 2 * SEQS, :] = value
    state[2 * SEQS :, :] = jnp.concatenate([inverse, gain[...], jnp.zeros((6, WIDTH), f32)], axis=0)
    lift[...] = (value * gain[...]).astype(bf16)
    short = value.astype(bf16)
    where = to_col(position[...].astype(f32), Q_DEV)
    high = jnp.floor(where * (1.0 / 32.0))
    lane = iota((Q_DEV, 128), 1)
    where = jnp.where(lane == 0, high, jnp.where(lane == 1, where - 32.0 * high, 0.0))
    q_pay[:, :, :WIDTH] = jnp.broadcast_to(short[None, :Q_DEV], (N_ROW, Q_DEV, WIDTH))
    q_pay[:, :, WIDTH:] = jnp.broadcast_to(where.astype(bf16)[None], (N_ROW, Q_DEV, 128))
    p_pay[...] = jnp.broadcast_to(short[None, Q_DEV:], (N_COL, P_DEV, WIDTH))


def lift_kernel(low, pooled, weight, out):
    out[:TOKENS, :] = dot(low[...], weight[...], ((1,), (1,))).astype(bf16)
    out[TOKENS:, :] = dot(pooled[...], weight[...], ((1,), (1,))).astype(bf16)


def score_kernel(q_all, p_all, state, lift, low, payload, position):
    order = row_order()
    q_rows = dot(order, q_all[...].reshape(ROWS, WIDTH + 128))
    position[...] = q_rows[:, WIDTH:]
    q_rows = q_rows[:, :WIDTH]
    p_cols = p_all[...].reshape(COLS, WIDTH)
    scores = dot(q_rows.astype(bf16), p_cols, ((1,), (1,)))
    payload[:, :, :COLS] = scores.reshape(NT, SHARE, COLS)
    q_sq = to_row(jnp.sum(q_rows * q_rows, axis=1, keepdims=True), ROWS)
    p_wide = p_cols.astype(f32)
    p_sq = jnp.sum(p_wide * p_wide, axis=1, keepdims=True)
    own = state[SEQS : 2 * SEQS, :]
    own_sq = to_row(jnp.sum(own * own, axis=1, keepdims=True), SEQS)
    cross = dot(lift[...], low[...], ((1,), (1,)))
    cross = jnp.sum(jnp.where(seg_mask(), cross, 0.0), axis=0, keepdims=True)
    rows = [to_row(p_sq[b * 128 : (b + 1) * 128], 128) for b in range(COLS // 128)]
    rows += [cross[:, b * 128 : (b + 1) * 128] for b in range(TOKENS // 128)]
    rows.append(jnp.concatenate([own_sq, jnp.zeros((1, 128 - SEQS), f32)], axis=1))
    rows.append(jnp.concatenate([q_sq, jnp.zeros((1, 128 - ROWS), f32)], axis=1))
    payload[:, :, COLS:] = jnp.broadcast_to(jnp.concatenate(rows, axis=0)[None], (NT, 8, 128))


def at_positive(position, x):
    where = position[:, 0:1] * 32.0 + position[:, 1:2]
    col = iota((position.shape[0], COLS), 1)
    passage = (col // 32) * 128 + x * 32 + col % 32
    return passage.astype(f32) == where


def softmax_kernel(ids, tile_mask, parts, position, payload, side):
    me, z, x = ids[1], ids[2], ids[3]
    total = jnp.sum(parts[...], axis=0)
    side[...] = total[:, COLS:]
    block = total[:, COLS:]
    scores = total[:, :COLS]
    p_sq = jnp.concatenate([block[0:1], block[1:2]], axis=1)
    own = iota((SHARE, 128), 1) == me * SHARE + iota((SHARE, 128), 0)
    q_sq = jnp.sum(jnp.where(own, block[7:8], 0.0), axis=1, keepdims=True)
    rn = lax.rsqrt(q_sq + EPS) * lax.rsqrt(p_sq + EPS)
    logits = LOGIT_SCALE * scores * rn
    block_of = iota((SHARE, COLS), 1) // 32
    allowed = jnp.zeros((SHARE, COLS), f32)
    for j in range(NZ):
        allowed = jnp.where(block_of == j, tile_mask[z, j].astype(f32), allowed)
    first = pl.multiple_of(me * SHARE, SHARE)
    is_pos = at_positive(position[pl.ds(first, SHARE), :], x)
    expo = jnp.exp(logits)
    others = jnp.where(is_pos, 0.0, expo * allowed)
    sums = [
        jnp.sum(others, axis=1, keepdims=True),
        jnp.sum(jnp.where(is_pos, expo, 0.0), axis=1, keepdims=True),
        jnp.sum(jnp.where(is_pos, logits, 0.0), axis=1, keepdims=True),
    ]
    lane = iota((SHARE, COLS), 1)
    row = jnp.zeros((SHARE, COLS), f32)
    for i, value in enumerate(sums):
        high, rest = split(value)
        middle, low = split(rest)
        for j, piece in enumerate((high, middle, low)):
            row = jnp.where(lane == 3 * i + j, piece, row)
    terms = rn * jnp.where(is_pos, 1.0, others)
    payload[...] = jnp.broadcast_to(
        jnp.concatenate([terms, row], axis=0).astype(bf16)[None], payload.shape
    )


def query_kernel(ids, parts, q_all, p_all, payload, terms_out):
    x = ids[3]
    value = parts[...].astype(f32)
    order = row_order()
    terms = value[:, :SHARE, :].reshape(ROWS, COLS).astype(bf16)
    terms = dot(order, terms, ((0,), (0,)))
    sums = value[:, SHARE:, :128].reshape(ROWS, 128).astype(bf16)
    sums = dot(order, sums, ((0,), (0,)))
    low = terms.astype(bf16)
    terms_out[...] = low
    at_pos = at_positive(q_all[...].reshape(ROWS, WIDTH + 128)[:, WIDTH:].astype(f32), x)
    p_cols = p_all[...].reshape(COLS, WIDTH)
    others = dot(jnp.where(at_pos, 0.0, terms).astype(bf16), p_cols)
    positive = dot(jnp.where(at_pos, terms, 0.0).astype(bf16), p_cols)
    payload[:, :Q_DEV, :] = others.astype(bf16).reshape(N_ROW, Q_DEV, WIDTH)
    payload[:, Q_DEV : 2 * Q_DEV, :] = positive.astype(bf16).reshape(N_ROW, Q_DEV, WIDTH)
    sums = jnp.concatenate([sums[k * Q_DEV : (k + 1) * Q_DEV] for k in range(N_ROW)], axis=1)
    payload[:, 2 * Q_DEV :, :] = jnp.broadcast_to(sums.astype(bf16)[None], (N_ROW, Q_DEV, WIDTH))


def passage_kernel(ids, parts, terms, q_all, loss, back_q, payload):
    me, x = ids[1], ids[3]
    total = jnp.sum(parts[...].astype(f32), axis=0)
    sums = total[2 * Q_DEV :]
    sums = jnp.concatenate([sums[:, k * 128 : (k + 1) * 128] for k in range(N_ROW)], axis=0)
    lane = iota((ROWS, 128), 1)
    others, positive, logit = (
        jnp.sum(jnp.where(lane // 3 == i, sums, 0.0), axis=1, keepdims=True) for i in range(3)
    )
    denom = others + positive
    losses = jnp.log(denom) - logit
    mine = (iota((ROWS, 128), 0) == x * Q_DEV + me * PAIR + lane) & (lane < PAIR)
    loss[...] = jnp.broadcast_to(
        jnp.sum(jnp.where(mine, losses, 0.0), axis=0, keepdims=True), loss.shape
    )
    factor = LOSS_SCALE / denom
    own_factor = jnp.zeros((Q_DEV, 1), f32)
    own_others = jnp.zeros((Q_DEV, 1), f32)
    for k in range(N_ROW):
        rows = slice(k * Q_DEV, (k + 1) * Q_DEV)
        own_factor = jnp.where(x == k, factor[rows], own_factor)
        own_others = jnp.where(x == k, others[rows], own_others)
    back_q[...] = own_factor * (total[:Q_DEV] - own_others * total[Q_DEV : 2 * Q_DEV])
    q_wide = q_all[...].reshape(ROWS, WIDTH + 128)
    at_pos = at_positive(q_wide[:, WIDTH:].astype(f32), x)
    value = terms[...].astype(f32) * jnp.where(at_pos, -factor * others, factor)
    d_p = dot(value.astype(bf16), q_wide[:, :WIDTH], ((0,), (0,)))
    payload[...] = d_p.astype(bf16).reshape(N_COL, P_DEV, WIDTH)


def up_kernel(back_q, p_parts, state, low, weight, back_gain, payload):
    back = jnp.concatenate([back_q[...], jnp.sum(p_parts[...].astype(f32), axis=0)], axis=0)
    inner = to_row(jnp.sum(state[SEQS : 2 * SEQS, :] * back, axis=1, keepdims=True), SEQS)
    scaled = back * state[2 * SEQS + 1 : 2 * SEQS + 2, :]
    back_gain[...] = scaled
    scaled = scaled.astype(bf16)
    cross = dot(scaled, low[...], ((1,), (1,)))
    cross = jnp.sum(jnp.where(seg_mask(), cross, 0.0), axis=0, keepdims=True)
    inner = jnp.concatenate([inner, jnp.zeros((1, HW_DEV - SEQS), f32)], axis=1)
    rows = [cross[:, :HW_DEV], cross[:, HW_DEV:], inner, jnp.zeros((5, HW_DEV), f32)]
    side = jnp.concatenate(split(jnp.concatenate(rows, axis=0)), axis=0).astype(bf16)
    for n in range(NT):
        w = weight[n * HW_DEV : (n + 1) * HW_DEV, :]
        payload[n, :SEQS, :] = dot(scaled, w, ((1,), (1,))).astype(bf16)
        payload[n, SEQS:, :] = side


def stage_kernel(far, here):
    here[...] = far[...]


def final_kernel(parts, side, state, back_gain, hidden, lifted, d_res, d_ctx, res, ctx, sems):
    total = jnp.sum(parts[...].astype(f32), axis=0)
    rows = total[SEQS : SEQS + 8] + total[SEQS + 8 :]
    cross_back = jnp.concatenate([rows[0:1], rows[1:2]], axis=1)
    inner = rows[2:3, :SEQS]
    block = side[...]
    cross = jnp.concatenate([block[b : b + 1] for b in range(2, 6)], axis=1)
    ratio = to_col(inner / (block[6:7, :SEQS] + EPS), SEQS)
    lead = LOGIT_SCALE * state[:SEQS, :]
    inverse = state[2 * SEQS : 2 * SEQS + 1, :]
    gain = state[2 * SEQS + 1 : 2 * SEQS + 2, :]
    by_token = jnp.sum(lead * (cross_back - ratio * cross), axis=0, keepdims=True)
    trail = inverse * inverse * by_token / FULL
    d_pooled = back_gain[...] - ratio * (state[SEQS : 2 * SEQS, :] * gain)
    seq_up = total[:SEQS] - ratio * lifted[TOKENS:, :].astype(f32)
    lead_high, lead_rest = split(lead)
    both_high, both_rest = split(jnp.concatenate([d_pooled, seq_up], axis=1))
    leads = jnp.concatenate([lead_high, lead_rest, lead_high], axis=0).astype(bf16)
    both = jnp.concatenate([both_high, both_high, both_rest], axis=0).astype(bf16)
    copies = []
    for b in range(TOKENS // 128):
        part = slice(b * 128, (b + 1) * 128)
        spread = dot(leads[:, part], both, ((0,), (0,)))
        column = to_col(trail[:, part], 128)
        res[part, :] = (spread[:, :WIDTH] - column * hidden[part, :]).astype(bf16)
        ctx[part, :] = (spread[:, WIDTH:] - column * lifted[part, :].astype(f32)).astype(bf16)
        for i, (here, far) in enumerate(((res, d_res), (ctx, d_ctx))):
            copies.append(
                pltpu.make_async_copy(here.at[part, :], far.at[part, :], sems.at[2 * b + i])
            )
            copies[-1].start()
    for copy in copies:
        copy.wait()


VMEM = pl.BlockSpec()
ANY = pl.BlockSpec(memory_space=pl.ANY)
SMEM = pl.BlockSpec(memory_space=pltpu.SMEM)


def whole(*shape):
    return pl.BlockSpec(shape, lambda i: (0,) * len(shape))


def call(
    kernel,
    name,
    outs,
    args,
    scalars=0,
    flops=1 << 20,
    flags=0,
    anywhere=(),
    anywhere_out=False,
    scratch=(),
    **grid,
):
    out = [jax.ShapeDtypeStruct(shape, dtype) for shape, dtype in outs]
    if not grid:
        grid = dict(
            in_specs=[SMEM] * scalars
            + [ANY if i in anywhere else VMEM for i in range(scalars, len(args))],
            out_specs=[ANY if anywhere_out else VMEM] * (len(out) - flags) + [SMEM] * flags,
            scratch_shapes=list(scratch),
        )
    size = sum(a.size * a.dtype.itemsize for a in (*args, *out))
    return pl.pallas_call(
        kernel,
        out_shape=out,
        **grid,
        compiler_params=pltpu.CompilerParams(vmem_limit_bytes=10 << 20),
        cost_estimate=pl.CostEstimate(flops=flops, bytes_accessed=size, transcendentals=0),
        name=name,
    )(*args)


def exchange(parts, axes):
    return lax.all_to_all(parts, axes, 0, 0)


def hidden_all(ids, out_weight, residual, context):
    parts = []
    for first in (0, HALF):
        own = lax.all_gather(context[first : first + HALF], "yl", axis=1, tiled=True)
        parts.append((own, lax.ppermute(own, "core", [(0, 1), (1, 0)])))
    hidden_outs = [((HALF, WIDTH), f32), ((HALF, WIDTH), bf16)]
    hidden_a, low_a, squares = call(
        functools.partial(hidden_kernel, 0),
        "hidden_a",
        hidden_outs + [((8, 128), f32)],
        (ids, *parts[0], out_weight, residual),
        1,
        flops=2 * HALF * 2048 * WIDTH,
    )
    hidden_b, low_b, squares = call(
        functools.partial(hidden_kernel, 1),
        "hidden_b",
        hidden_outs + [((NT, 8, 128), f32)],
        (ids, *parts[1], out_weight, residual, squares),
        1,
        flops=2 * HALF * 2048 * WIDTH,
    )
    hidden = jnp.concatenate([hidden_a, hidden_b], axis=0)
    low = jnp.concatenate([low_a, low_b], axis=0)
    return hidden, low, squares


def hidden_few(ids, out_weight, residual, compacted, dest):
    own = lax.all_gather(compacted, "yl", axis=1, tiled=True)
    other = lax.ppermute(own, "core", [(0, 1), (1, 0)])
    return tuple(
        call(
            few_kernel,
            "hidden",
            [((TOKENS, WIDTH), f32), ((TOKENS, WIDTH), bf16), ((NT, 8, 128), f32)],
            (ids, own, other, out_weight, residual, dest),
            1,
            flops=2 * CAP * 2048 * WIDTH,
        )
    )


def body(
    context,
    residual,
    out_weight,
    final_norm_weight,
    query_lengths,
    passage_lengths,
    positive_index,
    tile_mask,
):
    me = lax.axis_index(T)
    ids = jnp.stack(
        [lax.axis_index("core"), me, lax.axis_index("z"), lax.axis_index("x")]
    ).astype(i32)
    gain = final_norm_weight.reshape(1, WIDTH)

    compacted, dest, fits = call(
        compact_kernel,
        "compact",
        [((CAP, HW_DEV), bf16), ((8, TOKENS), f32), ((1, 1), i32)],
        (query_lengths.reshape(1, Q_DEV), passage_lengths.reshape(1, P_DEV), context),
        flops=2 * CAP * TOKENS * HW_DEV,
        flags=1,
        anywhere=(0, 1, 2),
        scratch=[
            pltpu.VMEM((1, Q_DEV), i32),
            pltpu.VMEM((1, P_DEV), i32),
            pltpu.VMEM((TOKENS, HW_DEV), bf16),
            pltpu.SemaphoreType.DMA((3,)),
        ],
    )
    hidden, low, squares = lax.cond(
        fits[0, 0] == 1,
        functools.partial(hidden_few, ids, out_weight, residual, compacted, dest),
        functools.partial(hidden_all, ids, out_weight, residual, context),
    )
    squares = exchange(squares, T)

    state, lift, q_pay, p_pay = call(
        pool_kernel,
        "pool",
        [
            ((2 * SEQS + 8, WIDTH), f32),
            ((SEQS, WIDTH), bf16),
            ((N_ROW, Q_DEV, WIDTH + 128), bf16),
            ((N_COL, P_DEV, WIDTH), bf16),
        ],
        (
            squares,
            query_lengths.reshape(1, Q_DEV),
            passage_lengths.reshape(1, P_DEV),
            positive_index.reshape(1, Q_DEV),
            gain,
            hidden,
        ),
    )
    q_all = exchange(q_pay, ROW)
    (lifted,) = call(
        lift_kernel,
        "lift",
        [((TOKENS + SEQS, NT * HW_DEV), bf16)],
        (low, lift, out_weight),
        flops=2 * TOKENS * 2048 * WIDTH,
        grid=(NT // 2,),
        in_specs=[
            whole(TOKENS, WIDTH),
            whole(SEQS, WIDTH),
            pl.BlockSpec((2 * HW_DEV, WIDTH), lambda i: (i, 0)),
        ],
        out_specs=[pl.BlockSpec((TOKENS + SEQS, 2 * HW_DEV), lambda i: (0, i))],
    )
    p_all = exchange(p_pay, COL)

    payload, position = call(
        score_kernel,
        "score",
        [((NT, SHARE, COLS + 128), f32), ((ROWS, 128), f32)],
        (q_all, p_all, state, lift, low),
    )
    payload, lifted = lax.optimization_barrier((payload, lifted))
    lifted = lax.psum_scatter(lifted, T, scatter_dimension=1, tiled=True)
    payload, side = call(
        softmax_kernel,
        "softmax",
        [((NT, 2 * SHARE, COLS), bf16), ((SHARE, 128), f32)],
        (ids, tile_mask, exchange(payload, T), position),
        2,
    )
    payload, terms = call(
        query_kernel,
        "query",
        [((N_ROW, 3 * Q_DEV, WIDTH), bf16), ((ROWS, COLS), bf16)],
        (ids, exchange(payload, T), q_all, p_all),
        1,
    )
    loss, back_q, payload = call(
        passage_kernel,
        "passage",
        [((8, 128), f32), ((Q_DEV, WIDTH), f32), ((N_COL, P_DEV, WIDTH), bf16)],
        (ids, exchange(payload, ROW), terms, q_all),
        1,
    )
    query_loss = loss[0, :PAIR]
    back_gain, payload = call(
        up_kernel,
        "up",
        [((SEQS, WIDTH), f32), ((NT, SEQS + 16, HW_DEV), bf16)],
        (back_q, exchange(payload, COL), state, low, out_weight),
    )
    payload, lifted = lax.optimization_barrier((payload, lifted))
    (lifted,) = call(stage_kernel, "stage", [(lifted.shape, bf16)], (lifted,))
    residual_gradient, d_context = call(
        final_kernel,
        "final",
        [((TOKENS, WIDTH), bf16), ((TOKENS, HW_DEV), bf16)],
        (exchange(payload, T), side, state, back_gain, hidden, lifted),
        anywhere_out=True,
        scratch=[
            pltpu.VMEM((TOKENS, WIDTH), bf16),
            pltpu.VMEM((TOKENS, HW_DEV), bf16),
            pltpu.SemaphoreType.DMA((2 * (TOKENS // 128),)),
        ],
    )
    return (query_loss, residual_gradient, d_context)


def solution(mesh):
    fine = Mesh(
        mesh.devices.reshape(NZ, NX, NYH, NYL, NC), ("z", "x", "yh", "yl", "core")
    )
    dp = ("z", "x", "yh")
    in_specs = (
        P(dp, T),
        P(dp, T),
        P(None, T),
        P(T),
        P(dp),
        P(dp),
        P(dp),
        P(),
    )
    out_specs = (P(dp + T), P(dp, T), P(dp, T))
    return jax.shard_map(body, mesh=fine, in_specs=in_specs, out_specs=out_specs, check_vma=False)
```

```python
import functools

import jax
import jax.numpy as jnp
from jax import lax
from jax.experimental import pallas as pl
from jax.experimental.pallas import tpu as pltpu
from jax.sharding import Mesh
from jax.sharding import PartitionSpec as P

Q_DEV = 16
P_DEV = 16
SEQ_LEN = 16
SEQS = Q_DEV + P_DEV
TOKENS = SEQS * SEQ_LEN
HALF = TOKENS // 2

EPS = 1e-06
LOGIT_SCALE = 20.0
LOSS_SCALE = 1024.0

NZ, NX, NYH, NYL, NC = 8, 4, 2, 4, 2
NT = NYL * NC
T = ("yl", "core")
ROW = ("x",)
COL = ("z", "yh")
N_ROW = NX
N_COL = NZ * NYH
ROWS = N_ROW * Q_DEV
COLS = N_COL * P_DEV
SHARE = ROWS // NT
PAIR = Q_DEV // NT
HW_DEV = 256
WIDTH = 512
FULL = WIDTH * NT
CAP = 352
CAP_PAD = 384

f32 = jnp.float32
bf16 = jnp.bfloat16
i32 = jnp.int32


def dot(a, b, dims=((1,), (0,)), exact=False):
    return lax.dot_general(
        a,
        b,
        (dims, ((), ())),
        preferred_element_type=f32,
        precision=lax.Precision.HIGHEST if exact else None,
    )


def iota(shape, dim):
    return lax.broadcasted_iota(i32, shape, dim)


def to_col(row, n):
    eye = iota((n, n), 0) == iota((n, n), 1)
    return jnp.sum(jnp.where(eye, row, 0.0), axis=1, keepdims=True)


def to_row(col, n):
    eye = iota((n, n), 0) == iota((n, n), 1)
    return jnp.sum(jnp.where(eye, col, 0.0), axis=0, keepdims=True)


def seg_mask():
    return iota((SEQS, TOKENS), 1) // SEQ_LEN == iota((SEQS, TOKENS), 0)


def split(value):
    high = value.astype(bf16).astype(f32)
    return high, value - high


def row_order():
    shape = (ROWS, ROWS)
    here, there = iota(shape, 0), iota(shape, 1)
    k, x, j = here // SHARE, (here % SHARE) // PAIR, here % PAIR
    return (there == x * Q_DEV + k * PAIR + j).astype(f32).astype(bf16)


def hidden_kernel(last, ids, own, other, weight, residual, *refs):
    if last:
        before, hidden, low, payload = refs
    else:
        hidden, low, payload = refs
    core = ids[0]
    total = residual[HALF * last : HALF * (last + 1), :].astype(f32)
    for y in range(NYL):
        part = slice(y * HW_DEV, (y + 1) * HW_DEV)
        for ref, c in ((own, core), (other, 1 - core)):
            first = pl.multiple_of((y * NC + c) * HW_DEV, HW_DEV)
            total = total + dot(ref[:, part], weight[pl.ds(first, HW_DEV), :])
    hidden[...] = total
    low[...] = total.astype(bf16)
    square = jnp.sum(total * total, axis=1, keepdims=True)
    rows = [to_row(square[b * 128 : (b + 1) * 128], 128) for b in range(HALF // 128)]
    if last:
        rows = [before[0:1], before[1:2]] + rows + [jnp.zeros((4, 128), f32)]
        payload[...] = jnp.broadcast_to(jnp.concatenate(rows, axis=0)[None], (NT, 8, 128))
    else:
        payload[...] = jnp.concatenate(rows + [jnp.zeros((6, 128), f32)], axis=0)


def compact_kernel(lens, context, out, dest, fits, context_here, sems):
    fetch = pltpu.make_async_copy(context, context_here, sems.at[0])
    fetch.start()
    by_lane = lens[...].astype(f32)
    lengths = to_col(by_lane, SEQS)
    fits[0, 0] = (jnp.sum(by_lane) <= CAP).astype(i32)
    before = iota((SEQS, SEQS), 1) < iota((SEQS, SEQS), 0)
    first = jnp.sum(jnp.where(before, by_lane, 0.0), axis=1, keepdims=True)
    slot = (iota((SEQS, TOKENS), 1) % SEQ_LEN).astype(f32)
    row = jnp.where(seg_mask() & (slot < lengths), first + slot + 1.0, 0.0)
    row = jnp.sum(row, axis=0, keepdims=True) - 1.0
    dest[...] = jnp.broadcast_to(row, (8, TOKENS))
    chosen = (iota((CAP, TOKENS), 0).astype(f32) == row).astype(f32).astype(bf16)
    fetch.wait()
    out[...] = dot(chosen, context_here[...]).astype(bf16)


def few_kernel(ids, own, other, weight, residual, dest, hidden, low, payload):
    core = ids[0]
    total = jnp.zeros((CAP, WIDTH), f32)
    for y in range(NYL):
        part = slice(y * HW_DEV, (y + 1) * HW_DEV)
        for ref, c in ((own, core), (other, 1 - core)):
            first = pl.multiple_of((y * NC + c) * HW_DEV, HW_DEV)
            total = total + dot(ref[:, part], weight[pl.ds(first, HW_DEV), :])
    total = jnp.concatenate([total, jnp.zeros((CAP_PAD - CAP, WIDTH), f32)], axis=0)
    high, rest = split(total)
    high, rest = high.astype(bf16), rest.astype(bf16)
    rows = []
    for b in range(TOKENS // 128):
        part = slice(b * 128, (b + 1) * 128)
        column = to_col(dest[0:1, part], 128)
        chosen = (iota((128, CAP_PAD), 1).astype(f32) == column).astype(f32).astype(bf16)
        block = dot(chosen, high) + dot(chosen, rest) + residual[part, :].astype(f32)
        hidden[part, :] = block
        low[part, :] = block.astype(bf16)
        rows.append(to_row(jnp.sum(block * block, axis=1, keepdims=True), 128))
    rows = jnp.concatenate(rows + [jnp.zeros((4, 128), f32)], axis=0)
    payload[...] = jnp.broadcast_to(rows[None], (NT, 8, 128))


def pool_kernel(
    squares, lens, position, gain, hidden, state, lift, q_pay, p_pay
):
    total = jnp.sum(squares[...], axis=0)
    total = jnp.concatenate([total[b : b + 1] for b in range(TOKENS // 128)], axis=1)
    inverse = lax.rsqrt(total / FULL + EPS)
    lengths = to_col(lens[...].astype(f32), SEQS)
    slot = (iota((SEQS, TOKENS), 1) % SEQ_LEN).astype(f32)
    weight = jnp.where(seg_mask() & (slot < lengths), 1.0 / lengths, 0.0) * inverse
    high, rest = (piece.astype(bf16) for piece in split(weight))
    hidden_high, hidden_rest = (piece.astype(bf16) for piece in split(hidden[...]))
    both = dot(jnp.concatenate([high, rest], axis=0), hidden_high)
    value = (both[:SEQS] + both[SEQS:] + dot(high, hidden_rest)) * gain[...]
    state[:SEQS, :] = weight
    state[SEQS : 2 * SEQS, :] = value
    state[2 * SEQS :, :] = jnp.concatenate([inverse, gain[...], jnp.zeros((6, WIDTH), f32)], axis=0)
    lift[...] = (value * gain[...]).astype(bf16)
    short = value.astype(bf16)
    where = to_col(position[...].astype(f32), Q_DEV)
    high = jnp.floor(where * (1.0 / 32.0))
    lane = iota((Q_DEV, 128), 1)
    where = jnp.where(lane == 0, high, jnp.where(lane == 1, where - 32.0 * high, 0.0))
    q_pay[:, :, :WIDTH] = jnp.broadcast_to(short[None, :Q_DEV], (N_ROW, Q_DEV, WIDTH))
    q_pay[:, :, WIDTH:] = jnp.broadcast_to(where.astype(bf16)[None], (N_ROW, Q_DEV, 128))
    p_pay[...] = jnp.broadcast_to(short[None, Q_DEV:], (N_COL, P_DEV, WIDTH))


def lift_kernel(low, pooled, weight, out):
    out[:TOKENS, :] = dot(low[...], weight[...], ((1,), (1,))).astype(bf16)
    out[TOKENS:, :] = dot(pooled[...], weight[...], ((1,), (1,))).astype(bf16)


def score_kernel(q_all, p_all, state, lift, low, payload, position):
    order = row_order()
    q_rows = dot(order, q_all[...].reshape(ROWS, WIDTH + 128))
    position[...] = q_rows[:, WIDTH:]
    q_rows = q_rows[:, :WIDTH]
    p_cols = p_all[...].reshape(COLS, WIDTH)
    scores = dot(q_rows.astype(bf16), p_cols, ((1,), (1,)))
    payload[:, :, :COLS] = scores.reshape(NT, SHARE, COLS)
    q_sq = to_row(jnp.sum(q_rows * q_rows, axis=1, keepdims=True), ROWS)
    p_wide = p_cols.astype(f32)
    p_sq = jnp.sum(p_wide * p_wide, axis=1, keepdims=True)
    own = state[SEQS : 2 * SEQS, :]
    own_sq = to_row(jnp.sum(own * own, axis=1, keepdims=True), SEQS)
    cross = dot(lift[...], low[...], ((1,), (1,)))
    cross = jnp.sum(jnp.where(seg_mask(), cross, 0.0), axis=0, keepdims=True)
    rows = [to_row(p_sq[b * 128 : (b + 1) * 128], 128) for b in range(COLS // 128)]
    rows += [cross[:, b * 128 : (b + 1) * 128] for b in range(TOKENS // 128)]
    rows.append(jnp.concatenate([own_sq, jnp.zeros((1, 128 - SEQS), f32)], axis=1))
    rows.append(jnp.concatenate([q_sq, jnp.zeros((1, 128 - ROWS), f32)], axis=1))
    payload[:, :, COLS:] = jnp.broadcast_to(jnp.concatenate(rows, axis=0)[None], (NT, 8, 128))


def at_positive(position, x):
    where = position[:, 0:1] * 32.0 + position[:, 1:2]
    col = iota((position.shape[0], COLS), 1)
    passage = (col // 32) * 128 + x * 32 + col % 32
    return passage.astype(f32) == where


def softmax_kernel(ids, tile_mask, parts, position, payload, side):
    me, z, x = ids[1], ids[2], ids[3]
    total = jnp.sum(parts[...], axis=0)
    side[...] = total[:, COLS:]
    block = total[:, COLS:]
    scores = total[:, :COLS]
    p_sq = jnp.concatenate([block[0:1], block[1:2]], axis=1)
    own = iota((SHARE, 128), 1) == me * SHARE + iota((SHARE, 128), 0)
    q_sq = jnp.sum(jnp.where(own, block[7:8], 0.0), axis=1, keepdims=True)
    rn = lax.rsqrt(q_sq + EPS) * lax.rsqrt(p_sq + EPS)
    logits = LOGIT_SCALE * scores * rn
    block_of = iota((SHARE, COLS), 1) // 32
    allowed = jnp.zeros((SHARE, COLS), f32)
    for j in range(NZ):
        allowed = jnp.where(block_of == j, tile_mask[z, j].astype(f32), allowed)
    first = pl.multiple_of(me * SHARE, SHARE)
    is_pos = at_positive(position[pl.ds(first, SHARE), :], x)
    expo = jnp.exp(logits)
    others = jnp.where(is_pos, 0.0, expo * allowed)
    sums = [
        jnp.sum(others, axis=1, keepdims=True),
        jnp.sum(jnp.where(is_pos, expo, 0.0), axis=1, keepdims=True),
        jnp.sum(jnp.where(is_pos, logits, 0.0), axis=1, keepdims=True),
    ]
    lane = iota((SHARE, COLS), 1)
    row = jnp.zeros((SHARE, COLS), f32)
    for i, value in enumerate(sums):
        high, rest = split(value)
        middle, low = split(rest)
        for j, piece in enumerate((high, middle, low)):
            row = jnp.where(lane == 3 * i + j, piece, row)
    terms = rn * jnp.where(is_pos, 1.0, others)
    payload[...] = jnp.broadcast_to(
        jnp.concatenate([terms, row], axis=0).astype(bf16)[None], payload.shape
    )


def query_kernel(ids, parts, q_all, p_all, payload, terms_out):
    x = ids[3]
    value = parts[...].astype(f32)
    order = row_order()
    terms = value[:, :SHARE, :].reshape(ROWS, COLS).astype(bf16)
    terms = dot(order, terms, ((0,), (0,)))
    sums = value[:, SHARE:, :128].reshape(ROWS, 128).astype(bf16)
    sums = dot(order, sums, ((0,), (0,)))
    low = terms.astype(bf16)
    terms_out[...] = low
    at_pos = at_positive(q_all[...].reshape(ROWS, WIDTH + 128)[:, WIDTH:].astype(f32), x)
    p_cols = p_all[...].reshape(COLS, WIDTH)
    others = dot(jnp.where(at_pos, 0.0, terms).astype(bf16), p_cols)
    positive = dot(jnp.where(at_pos, terms, 0.0).astype(bf16), p_cols)
    payload[:, :Q_DEV, :] = others.astype(bf16).reshape(N_ROW, Q_DEV, WIDTH)
    payload[:, Q_DEV : 2 * Q_DEV, :] = positive.astype(bf16).reshape(N_ROW, Q_DEV, WIDTH)
    sums = jnp.concatenate([sums[k * Q_DEV : (k + 1) * Q_DEV] for k in range(N_ROW)], axis=1)
    payload[:, 2 * Q_DEV :, :] = jnp.broadcast_to(sums.astype(bf16)[None], (N_ROW, Q_DEV, WIDTH))


def passage_kernel(ids, parts, terms, q_all, loss, back_q, payload):
    me, x = ids[1], ids[3]
    total = jnp.sum(parts[...].astype(f32), axis=0)
    sums = total[2 * Q_DEV :]
    sums = jnp.concatenate([sums[:, k * 128 : (k + 1) * 128] for k in range(N_ROW)], axis=0)
    lane = iota((ROWS, 128), 1)
    others, positive, logit = (
        jnp.sum(jnp.where(lane // 3 == i, sums, 0.0), axis=1, keepdims=True) for i in range(3)
    )
    denom = others + positive
    losses = jnp.log(denom) - logit
    mine = (iota((ROWS, 128), 0) == x * Q_DEV + me * PAIR + lane) & (lane < PAIR)
    loss[...] = jnp.broadcast_to(
        jnp.sum(jnp.where(mine, losses, 0.0), axis=0, keepdims=True), loss.shape
    )
    factor = LOSS_SCALE / denom
    own_factor = jnp.zeros((Q_DEV, 1), f32)
    own_others = jnp.zeros((Q_DEV, 1), f32)
    for k in range(N_ROW):
        rows = slice(k * Q_DEV, (k + 1) * Q_DEV)
        own_factor = jnp.where(x == k, factor[rows], own_factor)
        own_others = jnp.where(x == k, others[rows], own_others)
    back_q[...] = own_factor * (total[:Q_DEV] - own_others * total[Q_DEV : 2 * Q_DEV])
    q_wide = q_all[...].reshape(ROWS, WIDTH + 128)
    at_pos = at_positive(q_wide[:, WIDTH:].astype(f32), x)
    value = terms[...].astype(f32) * jnp.where(at_pos, -factor * others, factor)
    d_p = dot(value.astype(bf16), q_wide[:, :WIDTH], ((0,), (0,)))
    payload[...] = d_p.astype(bf16).reshape(N_COL, P_DEV, WIDTH)


def up_kernel(back_q, p_parts, state, low, weight, back_gain, payload):
    back = jnp.concatenate([back_q[...], jnp.sum(p_parts[...].astype(f32), axis=0)], axis=0)
    inner = to_row(jnp.sum(state[SEQS : 2 * SEQS, :] * back, axis=1, keepdims=True), SEQS)
    scaled = back * state[2 * SEQS + 1 : 2 * SEQS + 2, :]
    back_gain[...] = scaled
    scaled = scaled.astype(bf16)
    cross = dot(scaled, low[...], ((1,), (1,)))
    cross = jnp.sum(jnp.where(seg_mask(), cross, 0.0), axis=0, keepdims=True)
    inner = jnp.concatenate([inner, jnp.zeros((1, HW_DEV - SEQS), f32)], axis=1)
    rows = [cross[:, :HW_DEV], cross[:, HW_DEV:], inner, jnp.zeros((5, HW_DEV), f32)]
    side = jnp.concatenate(split(jnp.concatenate(rows, axis=0)), axis=0).astype(bf16)
    wide = jnp.concatenate([scaled, jnp.zeros((128 - SEQS, WIDTH), bf16)], axis=0)
    for n in range(NT):
        w = weight[n * HW_DEV : (n + 1) * HW_DEV, :]
        block = jnp.transpose(dot(w, wide, ((1,), (1,))))
        payload[n, :SEQS, :] = block[:SEQS].astype(bf16)
        payload[n, SEQS:, :] = side


def stage_kernel(far, here):
    here[...] = far[...]


def final_kernel(parts, side, state, back_gain, hidden, lifted, d_res, d_ctx, res, ctx, sems):
    total = jnp.sum(parts[...].astype(f32), axis=0)
    rows = total[SEQS : SEQS + 8] + total[SEQS + 8 :]
    cross_back = jnp.concatenate([rows[0:1], rows[1:2]], axis=1)
    inner = rows[2:3, :SEQS]
    block = side[...]
    cross = jnp.concatenate([block[b : b + 1] for b in range(2, 6)], axis=1)
    ratio = to_col(inner / (block[6:7, :SEQS] + EPS), SEQS)
    lead = LOGIT_SCALE * state[:SEQS, :]
    inverse = state[2 * SEQS : 2 * SEQS + 1, :]
    gain = state[2 * SEQS + 1 : 2 * SEQS + 2, :]
    by_token = jnp.sum(lead * (cross_back - ratio * cross), axis=0, keepdims=True)
    trail = inverse * inverse * by_token / FULL
    d_pooled = back_gain[...] - ratio * (state[SEQS : 2 * SEQS, :] * gain)
    seq_up = total[:SEQS] - ratio * lifted[TOKENS:, :].astype(f32)
    lead_high, lead_rest = split(lead)
    both_high, both_rest = split(jnp.concatenate([d_pooled, seq_up], axis=1))
    leads = jnp.concatenate([lead_high, lead_rest, lead_high], axis=0).astype(bf16)
    both = jnp.concatenate([both_high, both_high, both_rest], axis=0).astype(bf16)
    copies = []
    for b in range(TOKENS // 128):
        part = slice(b * 128, (b + 1) * 128)
        spread = dot(leads[:, part], both, ((0,), (0,)))
        column = to_col(trail[:, part], 128)
        res[part, :] = (spread[:, :WIDTH] - column * hidden[part, :]).astype(bf16)
        ctx[part, :] = (spread[:, WIDTH:] - column * lifted[part, :].astype(f32)).astype(bf16)
        for i, (here, far) in enumerate(((res, d_res), (ctx, d_ctx))):
            copies.append(
                pltpu.make_async_copy(here.at[part, :], far.at[part, :], sems.at[2 * b + i])
            )
            copies[-1].start()
    for copy in copies:
        copy.wait()


VMEM = pl.BlockSpec()
ANY = pl.BlockSpec(memory_space=pl.ANY)
SMEM = pl.BlockSpec(memory_space=pltpu.SMEM)


def whole(*shape):
    return pl.BlockSpec(shape, lambda i: (0,) * len(shape))


def call(
    kernel,
    name,
    outs,
    args,
    scalars=0,
    flops=1 << 20,
    flags=0,
    anywhere=(),
    anywhere_out=False,
    scratch=(),
    **grid,
):
    out = [jax.ShapeDtypeStruct(shape, dtype) for shape, dtype in outs]
    if not grid:
        grid = dict(
            in_specs=[SMEM] * scalars
            + [ANY if i in anywhere else VMEM for i in range(scalars, len(args))],
            out_specs=[ANY if anywhere_out else VMEM] * (len(out) - flags) + [SMEM] * flags,
            scratch_shapes=list(scratch),
        )
    size = sum(a.size * a.dtype.itemsize for a in (*args, *out))
    return pl.pallas_call(
        kernel,
        out_shape=out,
        **grid,
        compiler_params=pltpu.CompilerParams(vmem_limit_bytes=10 << 20),
        cost_estimate=pl.CostEstimate(flops=flops, bytes_accessed=size, transcendentals=0),
        name=name,
    )(*args)


def exchange(parts, axes):
    return lax.all_to_all(parts, axes, 0, 0)


def hidden_all(ids, out_weight, residual, context):
    parts = []
    for first in (0, HALF):
        own = lax.all_gather(context[first : first + HALF], "yl", axis=1, tiled=True)
        parts.append((own, lax.ppermute(own, "core", [(0, 1), (1, 0)])))
    hidden_outs = [((HALF, WIDTH), f32), ((HALF, WIDTH), bf16)]
    hidden_a, low_a, squares = call(
        functools.partial(hidden_kernel, 0),
        "hidden_a",
        hidden_outs + [((8, 128), f32)],
        (ids, *parts[0], out_weight, residual),
        1,
        flops=2 * HALF * 2048 * WIDTH,
    )
    hidden_b, low_b, squares = call(
        functools.partial(hidden_kernel, 1),
        "hidden_b",
        hidden_outs + [((NT, 8, 128), f32)],
        (ids, *parts[1], out_weight, residual, squares),
        1,
        flops=2 * HALF * 2048 * WIDTH,
    )
    hidden = jnp.concatenate([hidden_a, hidden_b], axis=0)
    low = jnp.concatenate([low_a, low_b], axis=0)
    return hidden, low, squares


def hidden_few(ids, out_weight, residual, compacted, dest):
    own = lax.all_gather(compacted, "yl", axis=1, tiled=True)
    other = lax.ppermute(own, "core", [(0, 1), (1, 0)])
    return tuple(
        call(
            few_kernel,
            "hidden",
            [((TOKENS, WIDTH), f32), ((TOKENS, WIDTH), bf16), ((NT, 8, 128), f32)],
            (ids, own, other, out_weight, residual, dest),
            1,
            flops=2 * CAP * 2048 * WIDTH,
        )
    )


def body(
    context,
    residual,
    out_weight,
    final_norm_weight,
    query_lengths,
    passage_lengths,
    positive_index,
    tile_mask,
):
    me = lax.axis_index(T)
    ids = jnp.stack(
        [lax.axis_index("core"), me, lax.axis_index("z"), lax.axis_index("x")]
    ).astype(i32)
    gain = final_norm_weight.reshape(1, WIDTH)
    lengths = jnp.concatenate([query_lengths, passage_lengths]).reshape(1, SEQS)

    compacted, dest, fits = call(
        compact_kernel,
        "compact",
        [((CAP, HW_DEV), bf16), ((8, TOKENS), f32), ((1, 1), i32)],
        (lengths, context),
        flops=2 * CAP * TOKENS * HW_DEV,
        flags=1,
        anywhere=(1,),
        scratch=[
            pltpu.VMEM((TOKENS, HW_DEV), bf16),
            pltpu.SemaphoreType.DMA((1,)),
        ],
    )
    hidden, low, squares = lax.cond(
        fits[0, 0] == 1,
        functools.partial(hidden_few, ids, out_weight, residual, compacted, dest),
        functools.partial(hidden_all, ids, out_weight, residual, context),
    )
    squares = exchange(squares, T)

    state, lift, q_pay, p_pay = call(
        pool_kernel,
        "pool",
        [
            ((2 * SEQS + 8, WIDTH), f32),
            ((SEQS, WIDTH), bf16),
            ((N_ROW, Q_DEV, WIDTH + 128), bf16),
            ((N_COL, P_DEV, WIDTH), bf16),
        ],
        (
            squares,
            lengths,
            positive_index.reshape(1, Q_DEV),
            gain,
            hidden,
        ),
    )
    q_all = exchange(q_pay, ROW)
    (lifted,) = call(
        lift_kernel,
        "lift",
        [((TOKENS + SEQS, NT * HW_DEV), bf16)],
        (low, lift, out_weight),
        flops=2 * TOKENS * 2048 * WIDTH,
        grid=(NT // 2,),
        in_specs=[
            whole(TOKENS, WIDTH),
            whole(SEQS, WIDTH),
            pl.BlockSpec((2 * HW_DEV, WIDTH), lambda i: (i, 0)),
        ],
        out_specs=[pl.BlockSpec((TOKENS + SEQS, 2 * HW_DEV), lambda i: (0, i))],
    )
    p_all = exchange(p_pay, COL)

    payload, position = call(
        score_kernel,
        "score",
        [((NT, SHARE, COLS + 128), f32), ((ROWS, 128), f32)],
        (q_all, p_all, state, lift, low),
    )
    payload, lifted = lax.optimization_barrier((payload, lifted))
    lifted = lax.psum_scatter(lifted, T, scatter_dimension=1, tiled=True)
    payload, side = call(
        softmax_kernel,
        "softmax",
        [((NT, 2 * SHARE, COLS), bf16), ((SHARE, 128), f32)],
        (ids, tile_mask, exchange(payload, T), position),
        2,
    )
    payload, terms = call(
        query_kernel,
        "query",
        [((N_ROW, 3 * Q_DEV, WIDTH), bf16), ((ROWS, COLS), bf16)],
        (ids, exchange(payload, T), q_all, p_all),
        1,
    )
    loss, back_q, payload = call(
        passage_kernel,
        "passage",
        [((8, 128), f32), ((Q_DEV, WIDTH), f32), ((N_COL, P_DEV, WIDTH), bf16)],
        (ids, exchange(payload, ROW), terms, q_all),
        1,
    )
    query_loss = loss[0, :PAIR]
    back_gain, payload = call(
        up_kernel,
        "up",
        [((SEQS, WIDTH), f32), ((NT, SEQS + 16, HW_DEV), bf16)],
        (back_q, exchange(payload, COL), state, low, out_weight),
    )
    payload, lifted = lax.optimization_barrier((payload, lifted))
    (lifted,) = call(stage_kernel, "stage", [(lifted.shape, bf16)], (lifted,))
    residual_gradient, d_context = call(
        final_kernel,
        "final",
        [((TOKENS, WIDTH), bf16), ((TOKENS, HW_DEV), bf16)],
        (exchange(payload, T), side, state, back_gain, hidden, lifted),
        anywhere_out=True,
        scratch=[
            pltpu.VMEM((TOKENS, WIDTH), bf16),
            pltpu.VMEM((TOKENS, HW_DEV), bf16),
            pltpu.SemaphoreType.DMA((2 * (TOKENS // 128),)),
        ],
    )
    return (query_loss, residual_gradient, d_context)


def solution(mesh):
    fine = Mesh(
        mesh.devices.reshape(NZ, NX, NYH, NYL, NC), ("z", "x", "yh", "yl", "core")
    )
    dp = ("z", "x", "yh")
    in_specs = (
        P(dp, T),
        P(dp, T),
        P(None, T),
        P(T),
        P(dp),
        P(dp),
        P(dp),
        P(),
    )
    out_specs = (P(dp + T), P(dp, T), P(dp, T))
    return jax.shard_map(body, mesh=fine, in_specs=in_specs, out_specs=out_specs, check_vma=False)
```

```python
import functools

import jax
import jax.numpy as jnp
from jax import lax
from jax.experimental import pallas as pl
from jax.experimental.pallas import tpu as pltpu
from jax.sharding import Mesh
from jax.sharding import PartitionSpec as P

Q_DEV = 16
P_DEV = 16
SEQ_LEN = 16
SEQS = Q_DEV + P_DEV
TOKENS = SEQS * SEQ_LEN
HALF = TOKENS // 2

EPS = 1e-06
LOGIT_SCALE = 20.0
LOSS_SCALE = 1024.0

NZ, NX, NYH, NYL, NC = 8, 4, 2, 4, 2
NT = NYL * NC
T = ("yl", "core")
ROW = ("x",)
COL = ("z", "yh")
N_ROW = NX
N_COL = NZ * NYH
ROWS = N_ROW * Q_DEV
COLS = N_COL * P_DEV
SHARE = ROWS // NT
PAIR = Q_DEV // NT
HW_DEV = 256
WIDTH = 512
FULL = WIDTH * NT
CAP = 352
CAP_PAD = 384

f32 = jnp.float32
bf16 = jnp.bfloat16
i32 = jnp.int32


def dot(a, b, dims=((1,), (0,)), exact=False):
    return lax.dot_general(
        a,
        b,
        (dims, ((), ())),
        preferred_element_type=f32,
        precision=lax.Precision.HIGHEST if exact else None,
    )


def iota(shape, dim):
    return lax.broadcasted_iota(i32, shape, dim)


def to_col(row, n):
    eye = iota((n, n), 0) == iota((n, n), 1)
    return jnp.sum(jnp.where(eye, row, 0.0), axis=1, keepdims=True)


def to_row(col, n):
    eye = iota((n, n), 0) == iota((n, n), 1)
    return jnp.sum(jnp.where(eye, col, 0.0), axis=0, keepdims=True)


def seg_mask():
    return iota((SEQS, TOKENS), 1) // SEQ_LEN == iota((SEQS, TOKENS), 0)


def split(value):
    high = value.astype(bf16).astype(f32)
    return high, value - high


def row_order():
    shape = (ROWS, ROWS)
    here, there = iota(shape, 0), iota(shape, 1)
    k, x, j = here // SHARE, (here % SHARE) // PAIR, here % PAIR
    return (there == x * Q_DEV + k * PAIR + j).astype(f32).astype(bf16)


def hidden_kernel(last, ids, own, other, weight, residual, *refs):
    if last:
        before, hidden, low, payload = refs
    else:
        hidden, low, payload = refs
    core = ids[0]
    total = residual[HALF * last : HALF * (last + 1), :].astype(f32)
    for y in range(NYL):
        part = slice(y * HW_DEV, (y + 1) * HW_DEV)
        for ref, c in ((own, core), (other, 1 - core)):
            first = pl.multiple_of((y * NC + c) * HW_DEV, HW_DEV)
            total = total + dot(ref[:, part], weight[pl.ds(first, HW_DEV), :])
    hidden[...] = total
    low[...] = total.astype(bf16)
    square = jnp.sum(total * total, axis=1, keepdims=True)
    rows = [to_row(square[b * 128 : (b + 1) * 128], 128) for b in range(HALF // 128)]
    if last:
        rows = [before[0:1], before[1:2]] + rows + [jnp.zeros((4, 128), f32)]
        payload[...] = jnp.broadcast_to(jnp.concatenate(rows, axis=0)[None], (NT, 8, 128))
    else:
        payload[...] = jnp.concatenate(rows + [jnp.zeros((6, 128), f32)], axis=0)


def compact_kernel(lens, context, out, dest, fits, context_here, sems):
    fetch = pltpu.make_async_copy(context, context_here, sems.at[0])
    fetch.start()
    by_lane = lens[...].astype(f32)
    lengths = to_col(by_lane, SEQS)
    fits[0, 0] = (jnp.sum(by_lane) <= CAP).astype(i32)
    before = iota((SEQS, SEQS), 1) < iota((SEQS, SEQS), 0)
    first = jnp.sum(jnp.where(before, by_lane, 0.0), axis=1, keepdims=True)
    slot = (iota((SEQS, TOKENS), 1) % SEQ_LEN).astype(f32)
    row = jnp.where(seg_mask() & (slot < lengths), first + slot + 1.0, 0.0)
    row = jnp.sum(row, axis=0, keepdims=True) - 1.0
    dest[...] = jnp.broadcast_to(row, (8, TOKENS))
    chosen = (iota((CAP, TOKENS), 0).astype(f32) == row).astype(f32).astype(bf16)
    fetch.wait()
    out[...] = dot(chosen, context_here[...]).astype(bf16)


def few_kernel(ids, own, other, weight, residual, dest, hidden, low, payload):
    core = ids[0]
    total = jnp.zeros((CAP, WIDTH), f32)
    for y in range(NYL):
        part = slice(y * HW_DEV, (y + 1) * HW_DEV)
        for ref, c in ((own, core), (other, 1 - core)):
            first = pl.multiple_of((y * NC + c) * HW_DEV, HW_DEV)
            total = total + dot(ref[:, part], weight[pl.ds(first, HW_DEV), :])
    total = jnp.concatenate([total, jnp.zeros((CAP_PAD - CAP, WIDTH), f32)], axis=0)
    high, rest = split(total)
    high, rest = high.astype(bf16), rest.astype(bf16)
    rows = []
    for b in range(TOKENS // 128):
        part = slice(b * 128, (b + 1) * 128)
        column = to_col(dest[0:1, part], 128)
        chosen = (iota((128, CAP_PAD), 1).astype(f32) == column).astype(f32).astype(bf16)
        block = dot(chosen, high) + dot(chosen, rest) + residual[part, :].astype(f32)
        hidden[part, :] = block
        low[part, :] = block.astype(bf16)
        rows.append(to_row(jnp.sum(block * block, axis=1, keepdims=True), 128))
    rows = jnp.concatenate(rows + [jnp.zeros((4, 128), f32)], axis=0)
    payload[...] = jnp.broadcast_to(rows[None], (NT, 8, 128))


def pool_kernel(
    squares, lens, position, gain, hidden, state, lift, q_pay, p_pay
):
    total = jnp.sum(squares[...], axis=0)
    total = jnp.concatenate([total[b : b + 1] for b in range(TOKENS // 128)], axis=1)
    inverse = lax.rsqrt(total / FULL + EPS)
    lengths = to_col(lens[...].astype(f32), SEQS)
    slot = (iota((SEQS, TOKENS), 1) % SEQ_LEN).astype(f32)
    weight = jnp.where(seg_mask() & (slot < lengths), 1.0 / lengths, 0.0) * inverse
    high, rest = (piece.astype(bf16) for piece in split(weight))
    hidden_high, hidden_rest = (piece.astype(bf16) for piece in split(hidden[...]))
    both = dot(jnp.concatenate([high, rest], axis=0), hidden_high)
    value = (both[:SEQS] + both[SEQS:] + dot(high, hidden_rest)) * gain[...]
    state[:SEQS, :] = weight
    state[SEQS : 2 * SEQS, :] = value
    state[2 * SEQS :, :] = jnp.concatenate([inverse, gain[...], jnp.zeros((6, WIDTH), f32)], axis=0)
    lift[...] = (value * gain[...]).astype(bf16)
    short = value.astype(bf16)
    where = to_col(position[...].astype(f32), Q_DEV)
    high = jnp.floor(where * (1.0 / 32.0))
    lane = iota((Q_DEV, 128), 1)
    where = jnp.where(lane == 0, high, jnp.where(lane == 1, where - 32.0 * high, 0.0))
    q_pay[:, :WIDTH] = short[:Q_DEV]
    q_pay[:, WIDTH:] = where.astype(bf16)
    p_pay[...] = jnp.broadcast_to(short[None, Q_DEV:], (N_COL, P_DEV, WIDTH))


def lift_kernel(low, pooled, weight, out, weight_here, out_here, sems):
    blocks = [slice(n * 2 * HW_DEV, (n + 1) * 2 * HW_DEV) for n in range(NT // 2)]
    reads = [
        pltpu.make_async_copy(weight.at[part, :], weight_here.at[part, :], sems.at[0, n])
        for n, part in enumerate(blocks)
    ]
    writes = [
        pltpu.make_async_copy(out_here.at[:, part], out.at[:, part], sems.at[1, n])
        for n, part in enumerate(blocks)
    ]
    for read in reads:
        read.start()
    for read, write, part in zip(reads, writes, blocks):
        read.wait()
        block = weight_here[part, :]
        out_here[:TOKENS, part] = dot(low[...], block, ((1,), (1,))).astype(bf16)
        out_here[TOKENS:, part] = dot(pooled[...], block, ((1,), (1,))).astype(bf16)
        write.start()
    for write in writes:
        write.wait()


def score_kernel(ids, *refs):
    q_parts, (p_all, state, lift, low, payload, position, q_all, by_distance) = refs[:NX], refs[NX:]
    for r in range(NX):
        by_distance[r] = q_parts[r][...]
    for x in range(NX):
        q_all[x] = by_distance[(ids[3] - x + NX) % NX]
    order = row_order()
    q_rows = dot(order, q_all[...].reshape(ROWS, WIDTH + 128))
    position[...] = q_rows[:, WIDTH:]
    q_rows = q_rows[:, :WIDTH]
    p_cols = p_all[...].reshape(COLS, WIDTH)
    scores = dot(q_rows.astype(bf16), p_cols, ((1,), (1,)))
    payload[:, :, :COLS] = scores.reshape(NT, SHARE, COLS)
    q_sq = to_row(jnp.sum(q_rows * q_rows, axis=1, keepdims=True), ROWS)
    p_wide = p_cols.astype(f32)
    p_sq = jnp.sum(p_wide * p_wide, axis=1, keepdims=True)
    own = state[SEQS : 2 * SEQS, :]
    own_sq = to_row(jnp.sum(own * own, axis=1, keepdims=True), SEQS)
    cross = dot(lift[...], low[...], ((1,), (1,)))
    cross = jnp.sum(jnp.where(seg_mask(), cross, 0.0), axis=0, keepdims=True)
    rows = [to_row(p_sq[b * 128 : (b + 1) * 128], 128) for b in range(COLS // 128)]
    rows += [cross[:, b * 128 : (b + 1) * 128] for b in range(TOKENS // 128)]
    rows.append(jnp.concatenate([own_sq, jnp.zeros((1, 128 - SEQS), f32)], axis=1))
    rows.append(jnp.concatenate([q_sq, jnp.zeros((1, 128 - ROWS), f32)], axis=1))
    payload[:, :, COLS:] = jnp.broadcast_to(jnp.concatenate(rows, axis=0)[None], (NT, 8, 128))


def at_positive(position, x):
    where = position[:, 0:1] * 32.0 + position[:, 1:2]
    col = iota((position.shape[0], COLS), 1)
    passage = (col // 32) * 128 + x * 32 + col % 32
    return passage.astype(f32) == where


def softmax_kernel(ids, tile_mask, parts, position, payload, side):
    me, z, x = ids[1], ids[2], ids[3]
    total = jnp.sum(parts[...], axis=0)
    side[...] = total[:, COLS:]
    block = total[:, COLS:]
    scores = total[:, :COLS]
    p_sq = jnp.concatenate([block[0:1], block[1:2]], axis=1)
    own = iota((SHARE, 128), 1) == me * SHARE + iota((SHARE, 128), 0)
    q_sq = jnp.sum(jnp.where(own, block[7:8], 0.0), axis=1, keepdims=True)
    rn = lax.rsqrt(q_sq + EPS) * lax.rsqrt(p_sq + EPS)
    logits = LOGIT_SCALE * scores * rn
    block_of = iota((SHARE, COLS), 1) // 32
    allowed = jnp.zeros((SHARE, COLS), f32)
    for j in range(NZ):
        allowed = jnp.where(block_of == j, tile_mask[z, j].astype(f32), allowed)
    first = pl.multiple_of(me * SHARE, SHARE)
    is_pos = at_positive(position[pl.ds(first, SHARE), :], x)
    expo = jnp.exp(logits)
    others = jnp.where(is_pos, 0.0, expo * allowed)
    sums = [
        jnp.sum(others, axis=1, keepdims=True),
        jnp.sum(jnp.where(is_pos, expo, 0.0), axis=1, keepdims=True),
        jnp.sum(jnp.where(is_pos, logits, 0.0), axis=1, keepdims=True),
    ]
    lane = iota((SHARE, COLS), 1)
    row = jnp.zeros((SHARE, COLS), f32)
    for i, value in enumerate(sums):
        high, rest = split(value)
        middle, low = split(rest)
        for j, piece in enumerate((high, middle, low)):
            row = jnp.where(lane == 3 * i + j, piece, row)
    terms = rn * jnp.where(is_pos, 1.0, others)
    payload[...] = jnp.broadcast_to(
        jnp.concatenate([terms, row], axis=0).astype(bf16)[None], payload.shape
    )


def query_kernel(ids, parts, q_all, p_all, payload, terms_out):
    x = ids[3]
    value = parts[...].astype(f32)
    order = row_order()
    terms = value[:, :SHARE, :].reshape(ROWS, COLS).astype(bf16)
    terms = dot(order, terms, ((0,), (0,)))
    sums = value[:, SHARE:, :128].reshape(ROWS, 128).astype(bf16)
    sums = dot(order, sums, ((0,), (0,)))
    low = terms.astype(bf16)
    terms_out[...] = low
    at_pos = at_positive(q_all[...].reshape(ROWS, WIDTH + 128)[:, WIDTH:].astype(f32), x)
    p_cols = p_all[...].reshape(COLS, WIDTH)
    others = dot(jnp.where(at_pos, 0.0, terms).astype(bf16), p_cols)
    positive = dot(jnp.where(at_pos, terms, 0.0).astype(bf16), p_cols)
    payload[:, :Q_DEV, :] = others.astype(bf16).reshape(N_ROW, Q_DEV, WIDTH)
    payload[:, Q_DEV : 2 * Q_DEV, :] = positive.astype(bf16).reshape(N_ROW, Q_DEV, WIDTH)
    sums = jnp.concatenate([sums[k * Q_DEV : (k + 1) * Q_DEV] for k in range(N_ROW)], axis=1)
    payload[:, 2 * Q_DEV :, :] = jnp.broadcast_to(sums.astype(bf16)[None], (N_ROW, Q_DEV, WIDTH))


def passage_kernel(ids, parts, terms, q_all, loss, back_q, payload):
    me, x = ids[1], ids[3]
    total = jnp.sum(parts[...].astype(f32), axis=0)
    sums = total[2 * Q_DEV :]
    sums = jnp.concatenate([sums[:, k * 128 : (k + 1) * 128] for k in range(N_ROW)], axis=0)
    lane = iota((ROWS, 128), 1)
    others, positive, logit = (
        jnp.sum(jnp.where(lane // 3 == i, sums, 0.0), axis=1, keepdims=True) for i in range(3)
    )
    denom = others + positive
    losses = jnp.log(denom) - logit
    mine = (iota((ROWS, 128), 0) == x * Q_DEV + me * PAIR + lane) & (lane < PAIR)
    loss[...] = jnp.broadcast_to(
        jnp.sum(jnp.where(mine, losses, 0.0), axis=0, keepdims=True), loss.shape
    )
    factor = LOSS_SCALE / denom
    own_factor = jnp.zeros((Q_DEV, 1), f32)
    own_others = jnp.zeros((Q_DEV, 1), f32)
    for k in range(N_ROW):
        rows = slice(k * Q_DEV, (k + 1) * Q_DEV)
        own_factor = jnp.where(x == k, factor[rows], own_factor)
        own_others = jnp.where(x == k, others[rows], own_others)
    back_q[...] = own_factor * (total[:Q_DEV] - own_others * total[Q_DEV : 2 * Q_DEV])
    q_wide = q_all[...].reshape(ROWS, WIDTH + 128)
    at_pos = at_positive(q_wide[:, WIDTH:].astype(f32), x)
    value = terms[...].astype(f32) * jnp.where(at_pos, -factor * others, factor)
    d_p = dot(value.astype(bf16), q_wide[:, :WIDTH], ((0,), (0,)))
    payload[...] = d_p.astype(bf16).reshape(N_COL, P_DEV, WIDTH)


def up_kernel(back_q, p_parts, state, low, weight, back_gain, payload):
    back = jnp.concatenate([back_q[...], jnp.sum(p_parts[...].astype(f32), axis=0)], axis=0)
    inner = to_row(jnp.sum(state[SEQS : 2 * SEQS, :] * back, axis=1, keepdims=True), SEQS)
    scaled = back * state[2 * SEQS + 1 : 2 * SEQS + 2, :]
    back_gain[...] = scaled
    scaled = scaled.astype(bf16)
    cross = dot(scaled, low[...], ((1,), (1,)))
    cross = jnp.sum(jnp.where(seg_mask(), cross, 0.0), axis=0, keepdims=True)
    inner = jnp.concatenate([inner, jnp.zeros((1, HW_DEV - SEQS), f32)], axis=1)
    rows = [cross[:, :HW_DEV], cross[:, HW_DEV:], inner, jnp.zeros((5, HW_DEV), f32)]
    side = jnp.concatenate(split(jnp.concatenate(rows, axis=0)), axis=0).astype(bf16)
    wide = jnp.concatenate([scaled, jnp.zeros((128 - SEQS, WIDTH), bf16)], axis=0)
    for n in range(NT):
        w = weight[n * HW_DEV : (n + 1) * HW_DEV, :]
        block = jnp.transpose(dot(w, wide, ((1,), (1,))))
        payload[n, :SEQS, :] = block[:SEQS].astype(bf16)
        payload[n, SEQS:, :] = side


def stage_kernel(far, here):
    here[...] = far[...]


def final_kernel(parts, side, state, back_gain, hidden, lifted, d_res, d_ctx, res, ctx, sems):
    total = jnp.sum(parts[...].astype(f32), axis=0)
    rows = total[SEQS : SEQS + 8] + total[SEQS + 8 :]
    cross_back = jnp.concatenate([rows[0:1], rows[1:2]], axis=1)
    inner = rows[2:3, :SEQS]
    block = side[...]
    cross = jnp.concatenate([block[b : b + 1] for b in range(2, 6)], axis=1)
    ratio = to_col(inner / (block[6:7, :SEQS] + EPS), SEQS)
    lead = LOGIT_SCALE * state[:SEQS, :]
    inverse = state[2 * SEQS : 2 * SEQS + 1, :]
    gain = state[2 * SEQS + 1 : 2 * SEQS + 2, :]
    by_token = jnp.sum(lead * (cross_back - ratio * cross), axis=0, keepdims=True)
    trail = inverse * inverse * by_token / FULL
    d_pooled = back_gain[...] - ratio * (state[SEQS : 2 * SEQS, :] * gain)
    seq_up = total[:SEQS] - ratio * lifted[TOKENS:, :].astype(f32)
    lead_high, lead_rest = split(lead)
    both_high, both_rest = split(jnp.concatenate([d_pooled, seq_up], axis=1))
    leads = jnp.concatenate([lead_high, lead_rest, lead_high], axis=0).astype(bf16)
    both = jnp.concatenate([both_high, both_high, both_rest], axis=0).astype(bf16)
    copies = []
    for b in range(TOKENS // 128):
        part = slice(b * 128, (b + 1) * 128)
        spread = dot(leads[:, part], both, ((0,), (0,)))
        column = to_col(trail[:, part], 128)
        res[part, :] = (spread[:, :WIDTH] - column * hidden[part, :]).astype(bf16)
        ctx[part, :] = (spread[:, WIDTH:] - column * lifted[part, :].astype(f32)).astype(bf16)
        for i, (here, far) in enumerate(((res, d_res), (ctx, d_ctx))):
            copies.append(
                pltpu.make_async_copy(here.at[part, :], far.at[part, :], sems.at[2 * b + i])
            )
            copies[-1].start()
    for copy in copies:
        copy.wait()


VMEM = pl.BlockSpec()
ANY = pl.BlockSpec(memory_space=pl.ANY)
SMEM = pl.BlockSpec(memory_space=pltpu.SMEM)


def whole(*shape):
    return pl.BlockSpec(shape, lambda i: (0,) * len(shape))


def call(
    kernel,
    name,
    outs,
    args,
    scalars=0,
    flops=1 << 20,
    flags=0,
    anywhere=(),
    anywhere_out=False,
    scratch=(),
    **grid,
):
    out = [jax.ShapeDtypeStruct(shape, dtype) for shape, dtype in outs]
    if not grid:
        grid = dict(
            in_specs=[SMEM] * scalars
            + [ANY if i in anywhere else VMEM for i in range(scalars, len(args))],
            out_specs=[ANY if anywhere_out else VMEM] * (len(out) - flags) + [SMEM] * flags,
            scratch_shapes=list(scratch),
        )
    size = sum(a.size * a.dtype.itemsize for a in (*args, *out))
    return pl.pallas_call(
        kernel,
        out_shape=out,
        **grid,
        compiler_params=pltpu.CompilerParams(vmem_limit_bytes=10 << 20),
        cost_estimate=pl.CostEstimate(flops=flops, bytes_accessed=size, transcendentals=0),
        name=name,
    )(*args)


def exchange(parts, axes):
    return lax.all_to_all(parts, axes, 0, 0)


def hidden_all(ids, out_weight, residual, context):
    parts = []
    for first in (0, HALF):
        own = lax.all_gather(context[first : first + HALF], "yl", axis=1, tiled=True)
        parts.append((own, lax.ppermute(own, "core", [(0, 1), (1, 0)])))
    hidden_outs = [((HALF, WIDTH), f32), ((HALF, WIDTH), bf16)]
    hidden_a, low_a, squares = call(
        functools.partial(hidden_kernel, 0),
        "hidden_a",
        hidden_outs + [((8, 128), f32)],
        (ids, *parts[0], out_weight, residual),
        1,
        flops=2 * HALF * 2048 * WIDTH,
    )
    hidden_b, low_b, squares = call(
        functools.partial(hidden_kernel, 1),
        "hidden_b",
        hidden_outs + [((NT, 8, 128), f32)],
        (ids, *parts[1], out_weight, residual, squares),
        1,
        flops=2 * HALF * 2048 * WIDTH,
    )
    hidden = jnp.concatenate([hidden_a, hidden_b], axis=0)
    low = jnp.concatenate([low_a, low_b], axis=0)
    return hidden, low, squares


def hidden_few(ids, out_weight, residual, compacted, dest):
    own = lax.all_gather(compacted, "yl", axis=1, tiled=True)
    other = lax.ppermute(own, "core", [(0, 1), (1, 0)])
    return tuple(
        call(
            few_kernel,
            "hidden",
            [((TOKENS, WIDTH), f32), ((TOKENS, WIDTH), bf16), ((NT, 8, 128), f32)],
            (ids, own, other, out_weight, residual, dest),
            1,
            flops=2 * CAP * 2048 * WIDTH,
        )
    )


def body(
    context,
    residual,
    out_weight,
    final_norm_weight,
    query_lengths,
    passage_lengths,
    positive_index,
    tile_mask,
):
    me = lax.axis_index(T)
    ids = jnp.stack(
        [lax.axis_index("core"), me, lax.axis_index("z"), lax.axis_index("x")]
    ).astype(i32)
    gain = final_norm_weight.reshape(1, WIDTH)
    lengths = jnp.concatenate([query_lengths, passage_lengths]).reshape(1, SEQS)

    compacted, dest, fits = call(
        compact_kernel,
        "compact",
        [((CAP, HW_DEV), bf16), ((8, TOKENS), f32), ((1, 1), i32)],
        (lengths, context),
        flops=2 * CAP * TOKENS * HW_DEV,
        flags=1,
        anywhere=(1,),
        scratch=[
            pltpu.VMEM((TOKENS, HW_DEV), bf16),
            pltpu.SemaphoreType.DMA((1,)),
        ],
    )
    hidden, low, squares = lax.cond(
        fits[0, 0] == 1,
        functools.partial(hidden_few, ids, out_weight, residual, compacted, dest),
        functools.partial(hidden_all, ids, out_weight, residual, context),
    )
    squares = exchange(squares, T)

    state, lift, q_pay, p_pay = call(
        pool_kernel,
        "pool",
        [
            ((2 * SEQS + 8, WIDTH), f32),
            ((SEQS, WIDTH), bf16),
            ((Q_DEV, WIDTH + 128), bf16),
            ((N_COL, P_DEV, WIDTH), bf16),
        ],
        (
            squares,
            lengths,
            positive_index.reshape(1, Q_DEV),
            gain,
            hidden,
        ),
    )
    q_parts = [q_pay] + [
        lax.ppermute(q_pay, "x", [(x, (x + r) % NX) for x in range(NX)]) for r in range(1, NX)
    ]
    (lifted,) = call(
        lift_kernel,
        "lift",
        [((TOKENS + SEQS, NT * HW_DEV), bf16)],
        (low, lift, out_weight),
        flops=2 * TOKENS * 2048 * WIDTH,
        anywhere=(2,),
        anywhere_out=True,
        scratch=[
            pltpu.VMEM((NT * HW_DEV, WIDTH), bf16),
            pltpu.VMEM((TOKENS + SEQS, NT * HW_DEV), bf16),
            pltpu.SemaphoreType.DMA((2, NT // 2)),
        ],
    )
    p_all = exchange(p_pay, COL)

    payload, position, q_all = call(
        score_kernel,
        "score",
        [
            ((NT, SHARE, COLS + 128), f32),
            ((ROWS, 128), f32),
            ((N_ROW, Q_DEV, WIDTH + 128), bf16),
        ],
        (ids, *q_parts, p_all, state, lift, low),
        1,
        scratch=[pltpu.VMEM((N_ROW, Q_DEV, WIDTH + 128), bf16)],
    )
    payload, lifted = lax.optimization_barrier((payload, lifted))
    lifted = lax.psum_scatter(lifted, T, scatter_dimension=1, tiled=True)
    payload, side = call(
        softmax_kernel,
        "softmax",
        [((NT, 2 * SHARE, COLS), bf16), ((SHARE, 128), f32)],
        (ids, tile_mask, exchange(payload, T), position),
        2,
    )
    payload, terms = call(
        query_kernel,
        "query",
        [((N_ROW, 3 * Q_DEV, WIDTH), bf16), ((ROWS, COLS), bf16)],
        (ids, exchange(payload, T), q_all, p_all),
        1,
    )
    loss, back_q, payload = call(
        passage_kernel,
        "passage",
        [((8, 128), f32), ((Q_DEV, WIDTH), f32), ((N_COL, P_DEV, WIDTH), bf16)],
        (ids, exchange(payload, ROW), terms, q_all),
        1,
    )
    query_loss = loss[0, :PAIR]
    back_gain, payload = call(
        up_kernel,
        "up",
        [((SEQS, WIDTH), f32), ((NT, SEQS + 16, HW_DEV), bf16)],
        (back_q, exchange(payload, COL), state, low, out_weight),
    )
    payload, lifted = lax.optimization_barrier((payload, lifted))
    (lifted,) = call(stage_kernel, "stage", [(lifted.shape, bf16)], (lifted,))
    residual_gradient, d_context = call(
        final_kernel,
        "final",
        [((TOKENS, WIDTH), bf16), ((TOKENS, HW_DEV), bf16)],
        (exchange(payload, T), side, state, back_gain, hidden, lifted),
        anywhere_out=True,
        scratch=[
            pltpu.VMEM((TOKENS, WIDTH), bf16),
            pltpu.VMEM((TOKENS, HW_DEV), bf16),
            pltpu.SemaphoreType.DMA((2 * (TOKENS // 128),)),
        ],
    )
    return (query_loss, residual_gradient, d_context)


def solution(mesh):
    fine = Mesh(
        mesh.devices.reshape(NZ, NX, NYH, NYL, NC), ("z", "x", "yh", "yl", "core")
    )
    dp = ("z", "x", "yh")
    in_specs = (
        P(dp, T),
        P(dp, T),
        P(None, T),
        P(T),
        P(dp),
        P(dp),
        P(dp),
        P(),
    )
    out_specs = (P(dp + T), P(dp, T), P(dp, T))
    return jax.shard_map(body, mesh=fine, in_specs=in_specs, out_specs=out_specs, check_vma=False)
```
